256 devices in a mesh: wide: 32 (over x, z_lo, y), narrow: 8 (over z_hi, core).
Axes of the slice: x: 4, y: 4, z: 8 (z_hi: 4, z_lo: 2; z = z_hi * 2 + z_lo), core: 2. Of those that a mesh axis runs over, the one named last changes fastest.
Arguments:
- state: float32 [2, 33554432], P(None, ('wide', 'narrow')), may hold values from -6 to 6
- gates: float32 [3, 2, 2, 32, 32], replicated, may hold values from -0.75 to 0.75
- wide_gates: float32 [3, 2, 2, 32, 32], replicated, may hold values from -0.75 to 0.75
- angles: float32 [3, 8], replicated, may hold values from -3.140625 to 3.140625
- coupled: int32 [3, 8], replicated, may hold values from 0 to 16
- sliced_index: int32 [3, 8], replicated, may hold values from 0 to 13
- sliced_values: int32 [14], replicated, may hold values from 0 to 1
Outputs:
- evolved: float32 [2, 33554432], P(None, ('wide', 'narrow'))
The draws below stay inside these ranges and needn't reach their ends.
All inputs are finite; a program needn't handle non-finite values.
Results may differ from the reference program's by a relative error of at most 0.00018.
Values sent between devices are 32-bit elements; how exact they have to be, the bound alone decides.
A program may use at most 128 MiB of HBM per device.

```python
import jax
import jax.numpy as jnp
from jax import lax

QLOC = 17
AMPS = 131072
STATES = 33554432
LAYERS = 3
COUPLINGS = 8
SLICED = 14
GATE = 32
N_WIDE = 32
N_NARROW = 8


def plant(drawn, own_key, smallest, high):
    place = [jax.random.randint(jax.random.fold_in(own_key, axis), (), 0, length) for axis, length in enumerate(drawn.shape)]
    longest = drawn.shape.index(max(drawn.shape))
    beside = place[:longest] + [(place[longest] + 1) % drawn.shape[longest]] + place[longest + 1:]
    return drawn.at[tuple(place)].set(smallest).at[tuple(beside)].set(high)


def steps_of(own_key, shape, cuts, least, largest):
    def one(position, parts):
        draws = jax.random.uniform(jax.random.fold_in(jax.random.fold_in(own_key, 6), position), (parts,), jnp.float32, least / len(cuts), largest / len(cuts))
        return jnp.repeat(jnp.exp(draws), shape[position] // parts).reshape((-1,) + (1,) * (len(shape) - position - 1))

    factor_of = one(*cuts[0])
    for cut in cuts[1:]:
        factor_of = factor_of * one(*cut)
    return factor_of


def normal_values(rng, extent, deviation, bound, cuts=(), kind=jnp.bfloat16):
    result = deviation * jax.random.normal(rng, extent, jnp.float32)
    if cuts:
        result = result * steps_of(rng, extent, cuts, -0.22, 0.18)
    return jnp.clip(result, -bound, bound).astype(kind)


def setup_inputs(seed: int = 0) -> dict:
    arg_keys = jax.random.split(jax.random.key(seed), 8)
    state = normal_values(arg_keys[0], (2, STATES), 1.0, 6.0, ((1, 256),), jnp.float32)
    gates = normal_values(arg_keys[1], (LAYERS, 2, 2, GATE, GATE), (2 * GATE) ** -0.5, 0.75, (), jnp.float32)
    wide_gates = normal_values(arg_keys[2], (LAYERS, 2, 2, GATE, GATE), (2 * GATE) ** -0.5, 0.75, (), jnp.float32)
    angles = jnp.clip(jax.random.uniform(arg_keys[3], (LAYERS, COUPLINGS), jnp.float32, -3.140625, 3.140625), -3.140625, 3.140625)
    coupled = plant(jax.random.randint(arg_keys[4], (LAYERS, COUPLINGS), 0, QLOC), jax.random.fold_in(arg_keys[4], 1), 0, QLOC - 1).astype(jnp.int32)
    sliced_index = plant(jax.random.randint(arg_keys[5], (LAYERS, COUPLINGS), 0, SLICED), jax.random.fold_in(arg_keys[5], 1), 0, SLICED - 1).astype(jnp.int32)
    sliced_values = plant(jax.random.randint(arg_keys[6], (SLICED,), 0, 2), jax.random.fold_in(arg_keys[6], 1), 0, 1).astype(jnp.int32)
    return dict(state=state, gates=gates, wide_gates=wide_gates, angles=angles, coupled=coupled, sliced_index=sliced_index, sliced_values=sliced_values)


HIGHEST = lax.Precision.HIGHEST


def complex_apply(matrix, amplitudes, form):
    def product(left, right):
        return jnp.einsum(form, left, right, precision=HIGHEST)
    real_part = product(matrix[0], amplitudes[0]) - product(matrix[1], amplitudes[1])
    imag_part = product(matrix[0], amplitudes[1]) + product(matrix[1], amplitudes[0])
    return jnp.stack([real_part, imag_part])


def coupling_table(sliced_index, sliced_values):
    names = jnp.arange(sliced_values.shape[0], dtype=jnp.int32)
    picked = (sliced_index[..., None] == names).astype(jnp.int32) * sliced_values
    return jnp.sum(picked, axis=-1).astype(jnp.int32)


def apply_phase(amplitudes, logical, angle_row, coupled_row, value_row):
    phases = jnp.zeros(logical.shape, jnp.float32)
    for coupling in range(angle_row.shape[0]):
        chosen = jnp.right_shift(logical, coupled_row[coupling]) & 1
        phases = phases + angle_row[coupling] * (chosen * value_row[coupling]).astype(jnp.float32)
    cosine = jnp.cos(phases)
    sine_part = jnp.sin(phases)
    return jnp.stack([amplitudes[0] * cosine - amplitudes[1] * sine_part,
                      amplitudes[0] * sine_part + amplitudes[1] * cosine])


def reference(state, gates, wide_gates, angles, coupled, sliced_index, sliced_values):
    wide_count = N_WIDE
    narrow_count = N_NARROW
    wide_bits = wide_count.bit_length() - 1
    share = AMPS // narrow_count
    lowest = AMPS // 1024
    values = coupling_table(sliced_index, sliced_values)
    logical = jnp.arange(AMPS, dtype=jnp.int32)
    amplitudes = state.reshape(2, wide_count, narrow_count, AMPS)

    def regroup(field):
        shaped = field.reshape(2, wide_count, narrow_count, narrow_count, share)
        return shaped.transpose(0, 1, 3, 2, 4).reshape(2, wide_count, narrow_count, AMPS)

    for layer_index in range(LAYERS):
        amplitudes = apply_phase(amplitudes, logical, angles[layer_index], coupled[layer_index], values[layer_index])
        moved = regroup(amplitudes).reshape(2, wide_count, narrow_count, 32, AMPS // 32)
        moved = complex_apply(gates[layer_index, 0], moved, "ij,wnjb->wnib")
        amplitudes = regroup(moved.reshape(2, wide_count, narrow_count, AMPS))
        shaped = amplitudes.reshape(2, wide_count, narrow_count, 32, 32, lowest)
        amplitudes = complex_apply(gates[layer_index, 1], shaped, "ij,wnajb->wnaib").reshape(2, wide_count, narrow_count, AMPS)
        for gate_index in range(2):
            wide_bit = (2 * layer_index + gate_index) % wide_bits
            upper = wide_count >> (wide_bit + 1)
            lower = 1 << wide_bit
            shaped = amplitudes.reshape(2, upper, 2, lower, narrow_count, 64, 16, lowest)
            matrix = wide_gates[layer_index, gate_index].reshape(2, 2, 16, 2, 16)
            mixed = complex_apply(matrix, shaped, "pqrs,hrwnasb->hpwnaqb")
            amplitudes = mixed.reshape(2, wide_count, narrow_count, AMPS)
    return amplitudes.reshape(2, STATES)
```

```python
import functools

import jax
import jax.numpy as jnp
from jax import lax
from jax.experimental import pallas as pl
from jax.experimental.pallas import tpu as pltpu
from jax.sharding import PartitionSpec as P

HIGHEST = lax.Precision.HIGHEST
MESH = pl.DeviceIdType.MESH
PIECES = 4
LANES = 128
F32 = jnp.float32
BF16 = jnp.bfloat16


def iota(shape, axis):
    return lax.broadcasted_iota(jnp.int32, shape, axis)


def halves(value):
    high = value.astype(BF16)
    return high, (value - high.astype(F32)).astype(BF16)


def thirds(value, axis):
    high = value.astype(BF16)
    rest = value - high.astype(F32)
    middle = rest.astype(BF16)
    return jnp.concatenate([high, middle, (rest - middle.astype(F32)).astype(BF16)], axis=axis)


def dot(left, right):
    return jnp.dot(left, right, preferred_element_type=F32)


def one_hot(wanted, own):
    return jnp.where(wanted == own, 1.0, 0.0).astype(BF16)


def on_lanes(real, imag, taken, given, kept_in, kept_out):
    pair = jnp.concatenate([thirds(real, 0), thirds(imag, 0)], axis=1)
    spread = one_hot(iota((96, 256), 0) % 32, given(iota((96, 256), 1)))
    columns = lax.dot_general(pair, spread, (((0,), (0,)), ((), ())), preferred_element_type=F32)
    to_real = iota((32, 256), 1) % 2 == 0
    from_real, from_imag = columns[:32], columns[32:]
    mixed = jnp.concatenate(
        [jnp.where(to_real, from_real, from_imag), jnp.where(to_real, -from_imag, from_real)], axis=0
    )
    rows = iota((256, 192), 0)
    pick = one_hot(iota((256, 192), 1) % 64, (rows % 2) * 32 + taken(rows))
    full = dot(pick, thirds(mixed, 0))
    return jnp.where(kept_in(iota((256, 256), 0)) == kept_out(iota((256, 256), 1)), full, 0.0)


def middle_index(index):
    return (index // 2) % 32


def middle_kept(index):
    return index // 64


def wide_index(index):
    return (index // 128) * 16 + (index // 2) % 16


def wide_kept(index):
    return (index // 32) % 4


def inner_index(index):
    return ((index // 64) % 2) * 16 + (index // 2) % 16


def inner_kept(index):
    return (index // 128) * 2 + (index // 32) % 2


def kernel(
    state, gates, wide, angles, coupled, chosen, values, out,
    loaded, z_send, z_got, xy_send, xy_got, xy_back, xy_home, z_back, z_home, done,
    first_g, rest_g, top_g,
    load_sem, z_s, z_r, xy_s, xy_r, xyb_s, xyb_r, zb_s, zb_r,
):
    w = lax.axis_index("wide")
    n = lax.axis_index("narrow")
    x, y, low, core = w // 8, w % 4, (w // 4) % 2, n % 2
    z = (n // 2) * 2 + low
    z_slot = low * 8 + n
    z_name = z * 2 + core
    xy_name = x * 4 + y

    def z_peer(step):
        other = (z + step // 2) % 8
        side = (core + step) % 2
        lane = (other // 2) * 2 + side
        return (x * 8 + (other % 2) * 4 + y, lane), other * 2 + side, (other % 2) * 8 + lane

    def xy_peer(step):
        across, along = (x + step // 4) % 4, (y + step) % 4
        return (across * 8 + low * 4 + along, n), across * 4 + along

    barrier = pltpu.get_barrier_semaphore()

    @pl.loop(1, 16)
    def _(step):
        pl.semaphore_signal(barrier, inc=1, device_id=z_peer(step)[0], device_id_type=MESH)
        pl.semaphore_signal(barrier, inc=1, device_id=xy_peer(step)[0], device_id_type=MESH)

    load = pltpu.make_async_copy(state, loaded, load_sem)
    load.start()
    load.wait()

    @pl.loop(0, 16)
    def _(block):
        turned = loaded[pl.ds(pl.multiple_of(block * 128, 128), 128), :].T
        for piece in range(PIECES):
            for side in range(2):
                rows = ((block // 2) * 2 + side) * 32 + (block % 2) * 16
                first = piece * 32 + side * 16
                z_send[piece, pl.ds(pl.multiple_of(rows, 16), 16), :] = turned[first : first + 16]

    def slot(index):
        return pl.ds(pl.multiple_of(index * 32, 32), 32)

    pl.semaphore_wait(barrier, 30)

    for piece in range(PIECES):
        @pl.loop(1, 16)
        def _(step):
            device, name, _ = z_peer(step)
            pltpu.make_async_remote_copy(
                src_ref=z_send.at[piece, slot(name)],
                dst_ref=z_got.at[piece, slot(z_slot)],
                send_sem=z_s.at[piece],
                recv_sem=z_r.at[piece],
                device_id=device,
                device_id_type=MESH,
            ).start()

        z_got[piece, slot(z_slot), :] = z_send[piece, slot(z_name), :]

    def arrived(buffer, semaphore, piece):
        part = buffer.at[piece, pl.ds(0, 480)]
        pltpu.make_async_copy(part, part, semaphore.at[piece]).wait()

    row, lane = iota((8, 128), 0), iota((8, 128), 1)
    unmixed = z * 16384 + core * 16 + xy_name
    place = jnp.where(
        row < 3, (lane % 32) * 128, jnp.where(row < 6, (lane % 4) * 4096, unmixed + (lane % 4) * 32)
    )
    phases = jnp.zeros((8, 128), F32)
    for layer in range(3):
        for coupling in range(8):
            turn = angles[layer, coupling] * values[chosen[layer, coupling]].astype(F32)
            bit = jnp.right_shift(place, coupled[layer, coupling]) & 1
            counted = jnp.where((row == layer) | (row == layer + 3) | (row == 6), bit, 0)
            phases = phases + turn * counted.astype(F32)
    cosine, sine = jnp.cos(phases), jnp.sin(phases)

    def turned_gate(gate, layer, phase_row):
        real, imag = gate[layer, 0], gate[layer, 1]
        c = cosine[phase_row : phase_row + 1, :32]
        s = sine[phase_row : phase_row + 1, :32]
        return real * c - imag * s, real * s + imag * c

    for layer in range(3):
        real, imag = turned_gate(gates.at[:, 1], layer, layer)
        middle = on_lanes(real, imag, middle_index, middle_index, middle_kept, middle_kept)
        real, imag = wide[layer, 0, 0], wide[layer, 0, 1]
        if layer == 0:
            plain = on_lanes(real, imag, wide_index, inner_index, wide_kept, inner_kept)
            times_i = on_lanes(-imag, real, wide_index, inner_index, wide_kept, inner_kept)
            first = jnp.dot(middle, jnp.concatenate([plain, times_i], axis=1), precision=HIGHEST, preferred_element_type=F32)
            first_g[0], first_g[1] = halves(first)
        else:
            plain = on_lanes(real, imag, wide_index, wide_index, wide_kept, wide_kept)
            both = jnp.dot(middle, plain, precision=HIGHEST, preferred_element_type=F32)
            rest_g[2 * layer - 1, 0], rest_g[2 * layer - 1, 1] = halves(both)
        real, imag = wide[layer, 1, 0], wide[layer, 1, 1]
        if layer < 2:
            second = on_lanes(real, imag, wide_index, wide_index, wide_kept, wide_kept)
        else:
            second = on_lanes(real, imag, inner_index, wide_index, inner_kept, wide_kept)
        rest_g[2 * layer, 0], rest_g[2 * layer, 1] = halves(second)

    top = [turned_gate(gates.at[:, 0], layer, layer + 3) for layer in range(3)]
    product = jnp.concatenate(top[0], axis=0)
    for real, imag in top[1:]:
        whole = jnp.concatenate(
            [jnp.concatenate([real, -imag], axis=1), jnp.concatenate([imag, real], axis=1)], axis=0
        )
        product = jnp.dot(whole, product, precision=HIGHEST, preferred_element_type=F32)

    def top_index(index):
        return (index % 8) * 4 + ((index // 8) % 2) * 2 + (index // 16) % 2

    def on_rows(real, imag):
        pick = one_hot(iota((128, 96), 1) % 32, top_index(iota((128, 96), 0)))
        part = dot(pick, thirds(jnp.concatenate([real, imag], axis=1), 0))
        columns = iota((192, 256), 1)
        spread = one_hot(iota((192, 256), 0) % 64, ((columns // 32) % 2) * 32 + top_index(columns))
        full = dot(thirds(part, 1), spread)
        return jnp.where(iota((128, 256), 0) // 32 == iota((128, 256), 1) // 64, full, 0.0)

    top_plain = on_rows(product[:32], product[32:])
    top_times_i = on_rows(-product[32:], product[:32])
    for piece in range(PIECES):
        here = (row == 6) & (lane == piece)
        c = jnp.sum(jnp.where(here, cosine, 0.0))
        s = jnp.sum(jnp.where(here, sine, 0.0))
        top_g[piece, 0], top_g[piece, 1] = halves(c * top_plain + s * top_times_i)

    def regroup(source, target, piece):
        for outer in range(16):
            for half in range(2):
                target[piece, pl.ds(outer * 32 + half * 16, 16), :] = source[
                    piece, pl.ds(half * 16 + outer, 16, stride=32), :
                ]

    def send_xy(source, target, sent, got, piece):
        @pl.loop(1, 16)
        def _(step):
            device, name = xy_peer(step)
            pltpu.make_async_remote_copy(
                src_ref=source.at[piece, slot(name)],
                dst_ref=target.at[piece, slot(xy_name)],
                send_sem=sent.at[piece],
                recv_sem=got.at[piece],
                device_id=device,
                device_id_type=MESH,
            ).start()

        target[piece, slot(xy_name), :] = source[piece, slot(xy_name), :]

    def inward(piece):
        arrived(z_got, z_r, piece)
        regroup(z_got, xy_send, piece)
        send_xy(xy_send, xy_got, xy_s, xy_r, piece)

    def right(tiles, zeros, ones, high, low_part):
        both = jnp.concatenate(
            [jnp.concatenate([tiles[k] for k in zeros], axis=0), jnp.concatenate([tiles[k] for k in ones], axis=0)], axis=1
        )
        upper, lower = halves(both)
        return dot(upper, high) + (dot(lower, high) + dot(upper, low_part))

    def gates_on(piece):
        arrived(xy_got, xy_r, piece)
        tiles = [xy_got[piece, pl.ds(k * 8, 8), :] for k in range(64)]
        zeros = [k for k in range(64) if not k & 4]
        mixed = right(tiles, zeros, [k | 4 for k in zeros], first_g[0], first_g[1])
        found = {}
        for place, k in enumerate(zeros):
            for column in range(4):
                found[k, column] = mixed[place * 8 : place * 8 + 8, column * 128 : column * 128 + 128]
        tiles = [None] * 64
        groups = [k for k in range(64) if not k & 6]
        for start in (0, 8):
            columns = []
            for half in range(2):
                columns.append(
                    jnp.concatenate(
                        [
                            found[k | bit13 * 2, times_i * 2 + bit12]
                            for k in groups[start + 4 * half : start + 4 * half + 4]
                            for times_i in range(2)
                            for bit12 in range(2)
                            for bit13 in range(2)
                        ],
                        axis=0,
                    )
                )
            upper, lower = halves(jnp.concatenate(columns, axis=1))
            high, low_part = top_g[piece, 0], top_g[piece, 1]
            topped = dot(high, upper) + (dot(low_part, upper) + dot(high, lower))
            for half in range(2):
                for which, k in enumerate(groups[start + 4 * half : start + 4 * half + 4]):
                    for bit12 in range(2):
                        for bit13 in range(2):
                            at = which * 32 + bit12 * 16 + bit13 * 8
                            tiles[k | bit12 * 4 | bit13 * 2] = topped[at : at + 8, half * 128 : half * 128 + 128]
        for gate, mask in enumerate((8, 1, 16, 32, 4)):
            zeros = [k for k in range(64) if not k & mask]
            mixed = right(tiles, zeros, [k | mask for k in zeros], rest_g[gate, 0], rest_g[gate, 1])
            for place, k in enumerate(zeros):
                tiles[k] = mixed[place * 8 : place * 8 + 8, :128]
                tiles[k | mask] = mixed[place * 8 : place * 8 + 8, 128:]
        for k in range(64):
            xy_back[piece, pl.ds(k * 8, 8), :] = tiles[k]
        send_xy(xy_back, xy_home, xyb_s, xyb_r, piece)

    def outward(piece):
        arrived(xy_home, xyb_r, piece)
        regroup(xy_home, z_back, piece)

        @pl.loop(1, 16)
        def _(step):
            device, _, there = z_peer(step)
            pltpu.make_async_remote_copy(
                src_ref=z_back.at[piece, slot(there)],
                dst_ref=z_home.at[piece, slot(z_name)],
                send_sem=zb_s.at[piece],
                recv_sem=zb_r.at[piece],
                device_id=device,
                device_id_type=MESH,
            ).start()

        z_home[piece, slot(z_name), :] = z_back[piece, slot(z_slot), :]

    @pl.loop(0, PIECES + 2)
    def _(step):
        @pl.when(step < PIECES)
        def _():
            inward(step)

        @pl.when((step >= 1) & (step < PIECES + 1))
        def _():
            gates_on(step - 1)

        @pl.when(step >= 2)
        def _():
            outward(step - 2)

    for piece in range(PIECES):
        arrived(z_home, zb_r, piece)

    @pl.loop(0, 16)
    def _(block):
        parts = []
        for piece in range(PIECES):
            for side in range(2):
                rows = ((block // 2) * 2 + side) * 32 + (block % 2) * 16
                parts.append(z_home[piece, pl.ds(pl.multiple_of(rows, 16), 16), :])
        done[pl.ds(pl.multiple_of(block * 128, 128), 128), :] = jnp.concatenate(parts, axis=0).T

    store = pltpu.make_async_copy(done, out, load_sem)
    store.start()
    for piece in range(PIECES):
        arrived(z_send, z_s, piece)
        arrived(xy_send, xy_s, piece)
        arrived(xy_back, xyb_s, piece)
        arrived(z_back, zb_s, piece)
    store.wait()


def on_device(state, gates, wide_gates, angles, coupled, sliced_index, sliced_values):
    rows = state.size // LANES
    linear = state.reshape(2, rows // 2, LANES).transpose(1, 0, 2).reshape(rows, LANES)
    any_space = pl.BlockSpec(memory_space=pl.ANY)
    vmem = pl.BlockSpec(memory_space=pltpu.VMEM)
    smem = pl.BlockSpec(memory_space=pltpu.SMEM)
    whole = pltpu.VMEM((rows, LANES), F32)
    pieces = pltpu.VMEM((PIECES, rows // PIECES, LANES), F32)
    counts = pltpu.SemaphoreType.DMA((PIECES,))
    result = pl.pallas_call(
        kernel,
        out_shape=jax.ShapeDtypeStruct((rows, LANES), F32),
        in_specs=[any_space, vmem, vmem, smem, smem, smem, smem],
        out_specs=any_space,
        scratch_shapes=[
            whole, pieces, pieces, pieces, pieces, pieces, pieces, pieces, pieces, whole,
            pltpu.VMEM((2, 256, 512), BF16),
            pltpu.VMEM((5, 2, 256, 256), BF16),
            pltpu.VMEM((PIECES, 2, 128, 256), BF16),
            pltpu.SemaphoreType.DMA,
            counts, counts, counts, counts, counts, counts, counts, counts,
        ],
        compiler_params=pltpu.CompilerParams(
            collective_id=0, has_side_effects=True, vmem_limit_bytes=40 << 20
        ),
        cost_estimate=pl.CostEstimate(flops=1 << 31, bytes_accessed=1 << 21, transcendentals=0),
    )(linear, gates, wide_gates, angles, coupled, sliced_index, sliced_values)
    return result.reshape(rows // 2, 2, LANES).transpose(1, 0, 2).reshape(state.shape)


def solution(mesh):
    in_specs = (P(None, ("wide", "narrow")), P(), P(), P(), P(), P(), P())
    out_specs = P(None, ("wide", "narrow"))
    return jax.shard_map(
        on_device, mesh=mesh, in_specs=in_specs, out_specs=out_specs, check_vma=False
    )
```

```python
import functools

import jax
import jax.numpy as jnp
from jax import lax
from jax.experimental import pallas as pl
from jax.experimental.pallas import tpu as pltpu
from jax.sharding import PartitionSpec as P

HIGHEST = lax.Precision.HIGHEST
MESH = pl.DeviceIdType.MESH
PIECES = 4
EARLY = 2
LANES = 128
F32 = jnp.float32
BF16 = jnp.bfloat16


def iota(shape, axis):
    return lax.broadcasted_iota(jnp.int32, shape, axis)


def halves(value):
    high = value.astype(BF16)
    return high, (value - high.astype(F32)).astype(BF16)


def thirds(value, axis):
    high = value.astype(BF16)
    rest = value - high.astype(F32)
    middle = rest.astype(BF16)
    return jnp.concatenate([high, middle, (rest - middle.astype(F32)).astype(BF16)], axis=axis)


def dot(left, right):
    return jnp.dot(left, right, preferred_element_type=F32)


def one_hot(wanted, own):
    return jnp.where(wanted == own, 1.0, 0.0).astype(BF16)


def on_lanes(real, imag, taken, given, kept_in, kept_out):
    pair = jnp.concatenate([thirds(real, 0), thirds(imag, 0)], axis=1)
    spread = one_hot(iota((96, 256), 0) % 32, given(iota((96, 256), 1)))
    columns = lax.dot_general(pair, spread, (((0,), (0,)), ((), ())), preferred_element_type=F32)
    to_real = iota((32, 256), 1) % 2 == 0
    from_real, from_imag = columns[:32], columns[32:]
    mixed = jnp.concatenate(
        [jnp.where(to_real, from_real, from_imag), jnp.where(to_real, -from_imag, from_real)], axis=0
    )
    rows = iota((256, 192), 0)
    pick = one_hot(iota((256, 192), 1) % 64, (rows % 2) * 32 + taken(rows))
    full = dot(pick, thirds(mixed, 0))
    return jnp.where(kept_in(iota((256, 256), 0)) == kept_out(iota((256, 256), 1)), full, 0.0)


def middle_index(index):
    return (index // 2) % 32


def middle_kept(index):
    return index // 64


def wide_index(index):
    return (index // 128) * 16 + (index // 2) % 16


def wide_kept(index):
    return (index // 32) % 4


def inner_index(index):
    return ((index // 64) % 2) * 16 + (index // 2) % 16


def inner_kept(index):
    return (index // 128) * 2 + (index // 32) % 2


def kernel(
    state, gates_in, wide_in, angles_in, coupled_in, chosen_in, values_in, out,
    gates, wide, angles, coupled, chosen, values,
    loaded, z_send, z_got, xy_send, early, ready, mixed, late, xy_home, z_back, z_home,
    first_g, rest_g, top_g,
    load_sem, small_sems, z_s, z_r, xy_s, xy_r, xyb_s, xyb_r, zb_s, zb_r,
):
    w = lax.axis_index("wide")
    n = lax.axis_index("narrow")
    x, y, low, core = w // 8, w % 4, (w // 4) % 2, n % 2
    z = (n // 2) * 2 + low
    z_slot = low * 8 + n
    z_name = z * 2 + core
    xy_name = x * 4 + y

    def z_peer(step):
        other = (z + step // 2) % 8
        side = (core + step) % 2
        lane = (other // 2) * 2 + side
        return (x * 8 + (other % 2) * 4 + y, lane), other * 2 + side, (other % 2) * 8 + lane

    def xy_peer(step):
        across, along = (x + step // 4) % 4, (y + step) % 4
        return (across * 8 + low * 4 + along, n), across * 4 + along

    barrier = pltpu.get_barrier_semaphore()

    @pl.loop(1, 16)
    def _(step):
        pl.semaphore_signal(barrier, inc=1, device_id=z_peer(step)[0], device_id_type=MESH)
        pl.semaphore_signal(barrier, inc=1, device_id=xy_peer(step)[0], device_id_type=MESH)

    load = pltpu.make_async_copy(state, loaded, load_sem)
    load.start()
    small = [
        pltpu.make_async_copy(source, target, small_sems.at[place])
        for place, (source, target) in enumerate(
            [
                (gates_in, gates), (wide_in, wide), (angles_in, angles),
                (coupled_in, coupled), (chosen_in, chosen), (values_in, values),
            ]
        )
    ]
    for copy in small:
        copy.start()
    load.wait()

    @pl.loop(0, 16, unroll=16)
    def _(block):
        turned = loaded[pl.ds(pl.multiple_of(block * 128, 128), 128), :].T
        for piece in range(PIECES):
            for side in range(2):
                name, half = (block // 2) * 2 + side, (block % 2) * 16
                first = piece * 32 + side * 16
                if piece == EARLY:
                    rows = pl.ds(half + name, 16, stride=32)
                    xy_send[piece, rows, :] = turned[first : first + 16]
                else:
                    rows = pl.ds(pl.multiple_of(name * 32 + half, 16), 16)
                    z_send[piece, rows, :] = turned[first : first + 16]

    def slot(index):
        return pl.ds(pl.multiple_of(index * 32, 32), 32)

    pl.semaphore_wait(barrier, 30)

    def send_z(source, target, sent, got, piece, inward):
        @pl.loop(1, 16)
        def _(step):
            device, name, there = z_peer(step)
            pltpu.make_async_remote_copy(
                src_ref=source.at[piece, slot(name if inward else there)],
                dst_ref=target.at[piece, slot(z_slot if inward else z_name)],
                send_sem=sent.at[piece],
                recv_sem=got.at[piece],
                device_id=device,
                device_id_type=MESH,
            ).start()

        own, landing = (z_name, z_slot) if inward else (z_slot, z_name)
        target[piece, slot(landing), :] = source[piece, slot(own), :]

    def send_xy(source, at, target, to, sent, got, piece):
        @pl.loop(1, 16)
        def _(step):
            device, name = xy_peer(step)
            pltpu.make_async_remote_copy(
                src_ref=source.at[at, slot(name)],
                dst_ref=target.at[to, slot(xy_name)],
                send_sem=sent.at[piece],
                recv_sem=got.at[piece],
                device_id=device,
                device_id_type=MESH,
            ).start()

        target[to, slot(xy_name), :] = source[at, slot(xy_name), :]

    def arrived(buffer, semaphore, piece):
        part = buffer.at[0, pl.ds(0, 480)]
        pltpu.make_async_copy(part, part, semaphore.at[piece]).wait()

    def regroup(source, at, target, to):
        for outer in range(16):
            for half in range(2):
                target[to, pl.ds(outer * 32 + half * 16, 16), :] = source[
                    at, pl.ds(half * 16 + outer, 16, stride=32), :
                ]

    send_z(z_send, z_got, z_s, z_r, 0, True)
    send_xy(xy_send, EARLY, early, 0, xy_s, xy_r, EARLY)
    send_z(z_send, z_got, z_s, z_r, 1, True)
    send_z(z_send, z_got, z_s, z_r, 3, True)

    for copy in small:
        copy.wait()
    row, lane = iota((8, 128), 0), iota((8, 128), 1)
    unmixed = z * 16384 + core * 16 + xy_name
    place = jnp.where(
        row < 3, (lane % 32) * 128, jnp.where(row < 6, (lane % 4) * 4096, unmixed + (lane % 4) * 32)
    )
    phases = jnp.zeros((8, 128), F32)
    for layer in range(3):
        for coupling in range(8):
            turn = angles[layer, coupling] * values[chosen[layer, coupling]].astype(F32)
            bit = jnp.right_shift(place, coupled[layer, coupling]) & 1
            counted = jnp.where((row == layer) | (row == layer + 3) | (row == 6), bit, 0)
            phases = phases + turn * counted.astype(F32)
    cosine, sine = jnp.cos(phases), jnp.sin(phases)

    def turned_gate(gate, layer, phase_row):
        real, imag = gate[layer, 0], gate[layer, 1]
        c = cosine[phase_row : phase_row + 1, :32]
        s = sine[phase_row : phase_row + 1, :32]
        return real * c - imag * s, real * s + imag * c

    for layer in range(3):
        real, imag = turned_gate(gates.at[:, 1], layer, layer)
        middle = on_lanes(real, imag, middle_index, middle_index, middle_kept, middle_kept)
        real, imag = wide[layer, 0, 0], wide[layer, 0, 1]
        if layer == 0:
            plain = on_lanes(real, imag, wide_index, inner_index, wide_kept, inner_kept)
            times_i = on_lanes(-imag, real, wide_index, inner_index, wide_kept, inner_kept)
            first = jnp.dot(middle, jnp.concatenate([plain, times_i], axis=1), precision=HIGHEST, preferred_element_type=F32)
            first_g[0], first_g[1] = halves(first)
        else:
            plain = on_lanes(real, imag, wide_index, wide_index, wide_kept, wide_kept)
            both = jnp.dot(middle, plain, precision=HIGHEST, preferred_element_type=F32)
            rest_g[2 * layer - 1, 0], rest_g[2 * layer - 1, 1] = halves(both)
        real, imag = wide[layer, 1, 0], wide[layer, 1, 1]
        if layer < 2:
            second = on_lanes(real, imag, wide_index, wide_index, wide_kept, wide_kept)
        else:
            second = on_lanes(real, imag, inner_index, wide_index, inner_kept, wide_kept)
        rest_g[2 * layer, 0], rest_g[2 * layer, 1] = halves(second)

    top = [turned_gate(gates.at[:, 0], layer, layer + 3) for layer in range(3)]
    product = jnp.concatenate(top[0], axis=0)
    for real, imag in top[1:]:
        whole = jnp.concatenate(
            [jnp.concatenate([real, -imag], axis=1), jnp.concatenate([imag, real], axis=1)], axis=0
        )
        product = jnp.dot(whole, product, precision=HIGHEST, preferred_element_type=F32)

    def top_index(index):
        return (index % 8) * 4 + ((index // 8) % 2) * 2 + (index // 16) % 2

    def on_rows(real, imag):
        pick = one_hot(iota((128, 96), 1) % 32, top_index(iota((128, 96), 0)))
        part = dot(pick, thirds(jnp.concatenate([real, imag], axis=1), 0))
        columns = iota((192, 256), 1)
        spread = one_hot(iota((192, 256), 0) % 64, ((columns // 32) % 2) * 32 + top_index(columns))
        full = dot(thirds(part, 1), spread)
        return jnp.where(iota((128, 256), 0) // 32 == iota((128, 256), 1) // 64, full, 0.0)

    top_plain = on_rows(product[:32], product[32:])
    top_times_i = on_rows(-product[32:], product[:32])
    for piece in range(PIECES):
        here = (row == 6) & (lane == piece)
        c = jnp.sum(jnp.where(here, cosine, 0.0))
        s = jnp.sum(jnp.where(here, sine, 0.0))
        top_g[piece, 0], top_g[piece, 1] = halves(c * top_plain + s * top_times_i)

    def right(tiles, zeros, ones, high, low_part):
        both = jnp.concatenate(
            [jnp.concatenate([tiles[k] for k in zeros], axis=0), jnp.concatenate([tiles[k] for k in ones], axis=0)], axis=1
        )
        upper, lower = halves(both)
        return dot(upper, high) + (dot(lower, high) + dot(upper, low_part))

    def gates_on(piece):
        tiles = [ready[piece, pl.ds(k * 8, 8), :] for k in range(64)]
        zeros = [k for k in range(64) if not k & 4]
        product = right(tiles, zeros, [k | 4 for k in zeros], first_g[0], first_g[1])
        found = {}
        for place, k in enumerate(zeros):
            for column in range(4):
                found[k, column] = product[place * 8 : place * 8 + 8, column * 128 : column * 128 + 128]
        tiles = [None] * 64
        groups = [k for k in range(64) if not k & 6]
        for start in (0, 8):
            columns = []
            for half in range(2):
                columns.append(
                    jnp.concatenate(
                        [
                            found[k | bit13 * 2, times_i * 2 + bit12]
                            for k in groups[start + 4 * half : start + 4 * half + 4]
                            for times_i in range(2)
                            for bit12 in range(2)
                            for bit13 in range(2)
                        ],
                        axis=0,
                    )
                )
            upper, lower = halves(jnp.concatenate(columns, axis=1))
            high, low_part = top_g[piece, 0], top_g[piece, 1]
            topped = dot(high, upper) + (dot(low_part, upper) + dot(high, lower))
            for half in range(2):
                for which, k in enumerate(groups[start + 4 * half : start + 4 * half + 4]):
                    for bit12 in range(2):
                        for bit13 in range(2):
                            at = which * 32 + bit12 * 16 + bit13 * 8
                            tiles[k | bit12 * 4 | bit13 * 2] = topped[at : at + 8, half * 128 : half * 128 + 128]
        for gate, mask in enumerate((8, 1, 16, 32, 4)):
            zeros = [k for k in range(64) if not k & mask]
            product = right(tiles, zeros, [k | mask for k in zeros], rest_g[gate, 0], rest_g[gate, 1])
            for place, k in enumerate(zeros):
                tiles[k] = product[place * 8 : place * 8 + 8, :128]
                tiles[k | mask] = product[place * 8 : place * 8 + 8, 128:]
        for k in range(64):
            mixed[piece, pl.ds(k * 8, 8), :] = tiles[k]

    def inward(piece):
        arrived(z_got, z_r, piece)
        regroup(z_got, piece, xy_send, piece)
        send_xy(xy_send, piece, ready, piece, xy_s, xy_r, piece)

    arrived(early, xy_r, EARLY)
    regroup(early, 0, z_send, EARLY)
    send_z(z_send, z_got, z_s, z_r, EARLY, True)

    @pl.loop(0, 2)
    def _(piece):
        inward(piece)

    @pl.loop(0, PIECES)
    def _(piece):
        @pl.when(piece == 1)
        def _():
            inward(3)

        @pl.when(piece == EARLY)
        def _():
            arrived(z_got, z_r, EARLY)
            regroup(z_got, EARLY, ready, EARLY)

        @pl.when(piece != EARLY)
        def _():
            arrived(ready, xy_r, piece)

        gates_on(piece)

        @pl.when(piece < 2)
        def _():
            regroup(mixed, piece, z_back, piece)
            send_z(z_back, z_home, zb_s, zb_r, piece, False)

        @pl.when(piece >= 2)
        def _():
            send_xy(mixed, piece, xy_home, piece, xyb_s, xyb_r, piece)

    def finish_late(piece):
        arrived(z_home, zb_r, piece)
        regroup(z_home, piece, late, piece)
        send_xy(late, piece, xy_home, piece, xyb_s, xyb_r, piece)

    finish_late(0)

    @pl.loop(2, PIECES)
    def _(piece):
        arrived(xy_home, xyb_r, piece)
        regroup(xy_home, piece, z_back, piece)
        send_z(z_back, z_home, zb_s, zb_r, piece, False)

    finish_late(1)
    for piece in range(2):
        arrived(xy_home, xyb_r, piece)
        arrived(z_home, zb_r, piece + 2)

    @pl.loop(0, 16, unroll=16)
    def _(block):
        parts = []
        for piece in range(PIECES):
            for side in range(2):
                name, half = (block // 2) * 2 + side, (block % 2) * 16
                if piece < 2:
                    parts.append(xy_home[piece, pl.ds(half + name, 16, stride=32), :])
                else:
                    parts.append(z_home[piece, pl.ds(pl.multiple_of(name * 32 + half, 16), 16), :])
        out[pl.ds(pl.multiple_of(block * 128, 128), 128), :] = jnp.concatenate(parts, axis=0).T

    for piece in range(PIECES):
        arrived(z_send, z_s, piece)
        arrived(xy_send, xy_s, piece)
        arrived(mixed, xyb_s, piece)
        arrived(z_back, zb_s, piece)


def on_device(state, gates, wide_gates, angles, coupled, sliced_index, sliced_values):
    rows = state.size // LANES
    linear = state.reshape(2, rows // 2, LANES).transpose(1, 0, 2).reshape(rows, LANES)
    hbm = pl.BlockSpec(memory_space=pltpu.HBM)
    whole = pltpu.VMEM((rows, LANES), F32)

    def pieces(count):
        return pltpu.VMEM((count, rows // PIECES, LANES), F32)

    counts = pltpu.SemaphoreType.DMA((PIECES,))
    result = pl.pallas_call(
        kernel,
        out_shape=pltpu.VMEM((rows, LANES), F32),
        in_specs=[hbm] * 7,
        out_specs=pl.BlockSpec(memory_space=pltpu.VMEM),
        scratch_shapes=[
            pltpu.VMEM(gates.shape, F32),
            pltpu.VMEM(wide_gates.shape, F32),
            pltpu.SMEM(angles.shape, F32),
            pltpu.SMEM(coupled.shape, jnp.int32),
            pltpu.SMEM(sliced_index.shape, jnp.int32),
            pltpu.SMEM(sliced_values.shape, jnp.int32),
            whole, pieces(4), pieces(4), pieces(4), pieces(1), pieces(4), pieces(4), pieces(2), pieces(4), pieces(4),
            pieces(4),
            pltpu.VMEM((2, 256, 512), BF16),
            pltpu.VMEM((5, 2, 256, 256), BF16),
            pltpu.VMEM((PIECES, 2, 128, 256), BF16),
            pltpu.SemaphoreType.DMA,
            pltpu.SemaphoreType.DMA((6,)),
            counts, counts, counts, counts, counts, counts, counts, counts,
        ],
        compiler_params=pltpu.CompilerParams(
            collective_id=0, has_side_effects=True, vmem_limit_bytes=48 << 20
        ),
        cost_estimate=pl.CostEstimate(flops=1 << 31, bytes_accessed=1 << 21, transcendentals=0),
    )(
        *(
            pltpu.with_memory_space_constraint(each, pltpu.HBM)
            for each in (linear, gates, wide_gates, angles, coupled, sliced_index, sliced_values)
        )
    )
    return result.reshape(rows // 2, 2, LANES).transpose(1, 0, 2).reshape(state.shape)


def solution(mesh):
    in_specs = (P(None, ("wide", "narrow")), P(), P(), P(), P(), P(), P())
    out_specs = P(None, ("wide", "narrow"))
    return jax.shard_map(
        on_device, mesh=mesh, in_specs=in_specs, out_specs=out_specs, check_vma=False
    )
```

```python
import functools

import jax
import jax.numpy as jnp
from jax import lax
from jax.experimental import pallas as pl
from jax.experimental.pallas import tpu as pltpu
from jax.sharding import PartitionSpec as P

HIGHEST = lax.Precision.HIGHEST
MESH = pl.DeviceIdType.MESH
PIECES = 4
LANES = 128
F32 = jnp.float32
BF16 = jnp.bfloat16


def iota(shape, axis):
    return lax.broadcasted_iota(jnp.int32, shape, axis)


def halves(value):
    high = value.astype(BF16)
    return high, (value - high.astype(F32)).astype(BF16)


def thirds(value, axis):
    high = value.astype(BF16)
    rest = value - high.astype(F32)
    middle = rest.astype(BF16)
    return jnp.concatenate([high, middle, (rest - middle.astype(F32)).astype(BF16)], axis=axis)


def dot(left, right):
    return jnp.dot(left, right, preferred_element_type=F32)


def one_hot(wanted, own):
    return jnp.where(wanted == own, 1.0, 0.0).astype(BF16)


def on_lanes(real, imag, taken, given, kept_in, kept_out):
    pair = jnp.concatenate([thirds(real, 0), thirds(imag, 0)], axis=1)
    spread = one_hot(iota((96, 256), 0) % 32, given(iota((96, 256), 1)))
    columns = lax.dot_general(pair, spread, (((0,), (0,)), ((), ())), preferred_element_type=F32)
    to_real = iota((32, 256), 1) % 2 == 0
    from_real, from_imag = columns[:32], columns[32:]
    mixed = jnp.concatenate(
        [jnp.where(to_real, from_real, from_imag), jnp.where(to_real, -from_imag, from_real)], axis=0
    )
    rows = iota((256, 192), 0)
    pick = one_hot(iota((256, 192), 1) % 64, (rows % 2) * 32 + taken(rows))
    full = dot(pick, thirds(mixed, 0))
    return jnp.where(kept_in(iota((256, 256), 0)) == kept_out(iota((256, 256), 1)), full, 0.0)


def middle_index(index):
    return (index // 2) % 32


def middle_kept(index):
    return index // 64


def wide_index(index):
    return (index // 128) * 16 + (index // 2) % 16


def wide_kept(index):
    return (index // 32) % 4


def inner_index(index):
    return ((index // 64) % 2) * 16 + (index // 2) % 16


def inner_kept(index):
    return (index // 128) * 2 + (index // 32) % 2


def kernel(
    state, gates_in, wide_in, angles_in, coupled_in, chosen_in, values_in, out,
    gates, wide, angles, coupled, chosen, values,
    loaded, z_send, z_got, xy_send, xy_got, ready, mixed, late, xy_home, z_back, z_home,
    first_g, rest_g, top_g,
    load_sems, small_sems, z_s, z_r, xy_s, xy_r, xyb_s, xyb_r, zb_s, zb_r,
):
    w = lax.axis_index("wide")
    n = lax.axis_index("narrow")
    x, y, low, core = w // 8, w % 4, (w // 4) % 2, n % 2
    z = (n // 2) * 2 + low
    z_slot = low * 8 + n
    z_name = z * 2 + core
    xy_name = x * 4 + y

    def z_peer(step):
        far = (step - 1) % 8
        other = (z + 4 + (1 - 2 * (far % 2)) * ((far + 1) // 2)) % 8
        side = (core + 1 + (step - 1) // 8) % 2
        lane = (other // 2) * 2 + side
        return (x * 8 + (other % 2) * 4 + y, lane), other * 2 + side, (other % 2) * 8 + lane

    def xy_peer(step):
        across, along = (x + step // 4) % 4, (y + step) % 4
        return (across * 8 + low * 4 + along, n), across * 4 + along

    barrier = pltpu.get_barrier_semaphore()

    loads = [
        pltpu.make_async_copy(
            state.at[pl.ds(part * 512, 512)], loaded.at[pl.ds(part * 512, 512)], load_sems.at[part]
        )
        for part in range(4)
    ]
    for load in loads:
        load.start()

    @pl.loop(1, 16)
    def _(step):
        pl.semaphore_signal(barrier, inc=1, device_id=z_peer(step)[0], device_id_type=MESH)

    @pl.loop(1, 16)
    def _(step):
        pl.semaphore_signal(barrier, inc=1, device_id=xy_peer(step)[0], device_id_type=MESH)

    small = [
        pltpu.make_async_copy(source, target, small_sems.at[place])
        for place, (source, target) in enumerate(
            [
                (gates_in, gates), (wide_in, wide), (angles_in, angles),
                (coupled_in, coupled), (chosen_in, chosen), (values_in, values),
            ]
        )
    ]
    for copy in small:
        copy.start()
    def turn(piece):
        loads[piece].wait()
        for block in range(4):
            start = piece * 512 + block * 128
            turned = loaded[start : start + 128, :].T
            for part in range(8):
                name, half = (block // 2) * 8 + part, (block % 2) * 16
                rows = turned[part * 16 : part * 16 + 16]
                if piece % 2:
                    xy_send[piece, pl.ds(half + name, 16, stride=32), :] = rows
                else:
                    z_send[piece, pl.ds(name * 32 + half, 16), :] = rows

    def slot(index):
        return pl.ds(pl.multiple_of(index * 32, 32), 32)


    def send_z(source, target, sent, got, piece, inward):
        @pl.loop(1, 16)
        def _(step):
            device, name, there = z_peer(step)
            pltpu.make_async_remote_copy(
                src_ref=source.at[piece, slot(name if inward else there)],
                dst_ref=target.at[piece, slot(z_slot if inward else z_name)],
                send_sem=sent.at[piece],
                recv_sem=got.at[piece],
                device_id=device,
                device_id_type=MESH,
            ).start()

        own, landing = (z_name, z_slot) if inward else (z_slot, z_name)
        target[piece, slot(landing), :] = source[piece, slot(own), :]

    def send_xy(source, target, sent, got, piece):
        @pl.loop(1, 16)
        def _(step):
            device, name = xy_peer(step)
            pltpu.make_async_remote_copy(
                src_ref=source.at[piece, slot(name)],
                dst_ref=target.at[piece, slot(xy_name)],
                send_sem=sent.at[piece],
                recv_sem=got.at[piece],
                device_id=device,
                device_id_type=MESH,
            ).start()

        target[piece, slot(xy_name), :] = source[piece, slot(xy_name), :]

    def arrived(buffer, semaphore, piece):
        part = buffer.at[0, pl.ds(0, 480)]
        pltpu.make_async_copy(part, part, semaphore.at[piece]).wait()

    def regroup(source, target, piece):
        for outer in range(16):
            for half in range(2):
                target[piece, pl.ds(outer * 32 + half * 16, 16), :] = source[
                    piece, pl.ds(half * 16 + outer, 16, stride=32), :
                ]

    turn(0)
    pl.semaphore_wait(barrier, 30)
    send_z(z_send, z_got, z_s, z_r, 0, True)
    for piece in range(1, PIECES):
        turn(piece)
    send_xy(xy_send, xy_got, xy_s, xy_r, 1)
    send_z(z_send, z_got, z_s, z_r, 2, True)
    send_xy(xy_send, xy_got, xy_s, xy_r, 3)

    for copy in small:
        copy.wait()
    row, lane = iota((8, 128), 0), iota((8, 128), 1)
    unmixed = (z_name // 8) * 16384 + (z_name % 8) * 16 + xy_name
    place = jnp.where(
        row < 3, (lane % 32) * 128, jnp.where(row < 6, (lane % 4) * 4096, unmixed + (lane % 4) * 32768)
    )
    phases = jnp.zeros((8, 128), F32)
    for layer in range(3):
        for coupling in range(8):
            turn = angles[layer, coupling] * values[chosen[layer, coupling]].astype(F32)
            bit = jnp.right_shift(place, coupled[layer, coupling]) & 1
            counted = jnp.where((row == layer) | (row == layer + 3) | (row == 6), bit, 0)
            phases = phases + turn * counted.astype(F32)
    cosine, sine = jnp.cos(phases), jnp.sin(phases)

    def turned_gate(gate, layer, phase_row):
        real, imag = gate[layer, 0], gate[layer, 1]
        c = cosine[phase_row : phase_row + 1, :32]
        s = sine[phase_row : phase_row + 1, :32]
        return real * c - imag * s, real * s + imag * c

    for layer in range(3):
        real, imag = turned_gate(gates.at[:, 1], layer, layer)
        middle = on_lanes(real, imag, middle_index, middle_index, middle_kept, middle_kept)
        real, imag = wide[layer, 0, 0], wide[layer, 0, 1]
        if layer == 0:
            plain = on_lanes(real, imag, wide_index, inner_index, wide_kept, inner_kept)
            times_i = on_lanes(-imag, real, wide_index, inner_index, wide_kept, inner_kept)
            first = jnp.dot(middle, jnp.concatenate([plain, times_i], axis=1), precision=HIGHEST, preferred_element_type=F32)
            first_g[0], first_g[1] = halves(first)
        else:
            plain = on_lanes(real, imag, wide_index, wide_index, wide_kept, wide_kept)
            both = jnp.dot(middle, plain, precision=HIGHEST, preferred_element_type=F32)
            rest_g[2 * layer - 1, 0], rest_g[2 * layer - 1, 1] = halves(both)
        real, imag = wide[layer, 1, 0], wide[layer, 1, 1]
        if layer < 2:
            second = on_lanes(real, imag, wide_index, wide_index, wide_kept, wide_kept)
        else:
            second = on_lanes(real, imag, inner_index, wide_index, inner_kept, wide_kept)
        rest_g[2 * layer, 0], rest_g[2 * layer, 1] = halves(second)

    top = [turned_gate(gates.at[:, 0], layer, layer + 3) for layer in range(3)]
    product = jnp.concatenate(top[0], axis=0)
    for real, imag in top[1:]:
        whole = jnp.concatenate(
            [jnp.concatenate([real, -imag], axis=1), jnp.concatenate([imag, real], axis=1)], axis=0
        )
        product = jnp.dot(whole, product, precision=HIGHEST, preferred_element_type=F32)

    def top_index(index):
        return (index % 8) * 4 + ((index // 8) % 2) * 2 + (index // 16) % 2

    def on_rows(real, imag):
        pick = one_hot(iota((128, 96), 1) % 32, top_index(iota((128, 96), 0)))
        part = dot(pick, thirds(jnp.concatenate([real, imag], axis=1), 0))
        columns = iota((192, 256), 1)
        spread = one_hot(iota((192, 256), 0) % 64, ((columns // 32) % 2) * 32 + top_index(columns))
        full = dot(thirds(part, 1), spread)
        return jnp.where(iota((128, 256), 0) // 32 == iota((128, 256), 1) // 64, full, 0.0)

    top_plain = on_rows(product[:32], product[32:])
    top_times_i = on_rows(-product[32:], product[:32])
    for piece in range(PIECES):
        here = (row == 6) & (lane == piece)
        c = jnp.sum(jnp.where(here, cosine, 0.0))
        s = jnp.sum(jnp.where(here, sine, 0.0))
        top_g[piece, 0], top_g[piece, 1] = halves(c * top_plain + s * top_times_i)

    def right(tiles, zeros, ones, high, low_part):
        both = jnp.concatenate(
            [jnp.concatenate([tiles[k] for k in zeros], axis=0), jnp.concatenate([tiles[k] for k in ones], axis=0)], axis=1
        )
        upper, lower = halves(both)
        return dot(upper, high) + (dot(lower, high) + dot(upper, low_part))

    def gates_on(piece):
        tiles = [ready[piece, pl.ds(k * 8, 8), :] for k in range(64)]
        zeros = [k for k in range(64) if not k & 4]
        product = right(tiles, zeros, [k | 4 for k in zeros], first_g[0], first_g[1])
        found = {}
        for place, k in enumerate(zeros):
            for column in range(4):
                found[k, column] = product[place * 8 : place * 8 + 8, column * 128 : column * 128 + 128]
        tiles = [None] * 64
        groups = [k for k in range(64) if not k & 6]
        for start in (0, 8):
            columns = []
            for half in range(2):
                columns.append(
                    jnp.concatenate(
                        [
                            found[k | bit13 * 2, times_i * 2 + bit12]
                            for k in groups[start + 4 * half : start + 4 * half + 4]
                            for times_i in range(2)
                            for bit12 in range(2)
                            for bit13 in range(2)
                        ],
                        axis=0,
                    )
                )
            upper, lower = halves(jnp.concatenate(columns, axis=1))
            high, low_part = top_g[piece, 0], top_g[piece, 1]
            topped = dot(high, upper) + (dot(low_part, upper) + dot(high, lower))
            for half in range(2):
                for which, k in enumerate(groups[start + 4 * half : start + 4 * half + 4]):
                    for bit12 in range(2):
                        for bit13 in range(2):
                            at = which * 32 + bit12 * 16 + bit13 * 8
                            tiles[k | bit12 * 4 | bit13 * 2] = topped[at : at + 8, half * 128 : half * 128 + 128]
        for gate, mask in enumerate((8, 1, 16, 32, 4)):
            zeros = [k for k in range(64) if not k & mask]
            product = right(tiles, zeros, [k | mask for k in zeros], rest_g[gate, 0], rest_g[gate, 1])
            for place, k in enumerate(zeros):
                tiles[k] = product[place * 8 : place * 8 + 8, :128]
                tiles[k | mask] = product[place * 8 : place * 8 + 8, 128:]
        for k in range(64):
            mixed[piece, pl.ds(k * 8, 8), :] = tiles[k]

    @pl.loop(0, PIECES, step=2)
    def _(piece):
        arrived(xy_got, xy_r, piece + 1)
        regroup(xy_got, z_send, piece + 1)
        send_z(z_send, z_got, z_s, z_r, piece + 1, True)
        arrived(z_got, z_r, piece)
        regroup(z_got, xy_send, piece)
        send_xy(xy_send, ready, xy_s, xy_r, piece)

    @pl.loop(0, PIECES)
    def _(piece):
        @pl.when(piece % 2 == 0)
        def _():
            arrived(ready, xy_r, piece)

        @pl.when(piece % 2 == 1)
        def _():
            arrived(z_got, z_r, piece)
            regroup(z_got, ready, piece)

        gates_on(piece)

        @pl.when(piece % 2 == 0)
        def _():
            regroup(mixed, z_back, piece)
            send_z(z_back, z_home, zb_s, zb_r, piece, False)

        @pl.when(piece % 2 == 1)
        def _():
            send_xy(mixed, xy_home, xyb_s, xyb_r, piece)

    @pl.loop(0, PIECES, step=2)
    def _(piece):
        arrived(xy_home, xyb_r, piece + 1)
        regroup(xy_home, z_back, piece + 1)
        send_z(z_back, z_home, zb_s, zb_r, piece + 1, False)
        arrived(z_home, zb_r, piece)
        regroup(z_home, late, piece)
        send_xy(late, xy_home, xyb_s, xyb_r, piece)

    for piece in range(PIECES):
        if piece % 2:
            arrived(z_home, zb_r, piece)
        else:
            arrived(xy_home, xyb_r, piece)
        for block in range(4):
            parts = []
            for part in range(8):
                name, half = (block // 2) * 8 + part, (block % 2) * 16
                if piece % 2:
                    parts.append(z_home[piece, pl.ds(name * 32 + half, 16), :])
                else:
                    parts.append(xy_home[piece, pl.ds(half + name, 16, stride=32), :])
            out[pl.ds(piece * 512 + block * 128, 128), :] = jnp.concatenate(parts, axis=0).T

    for piece in range(PIECES):
        arrived(z_send, z_s, piece)
        arrived(xy_send, xy_s, piece)
        arrived(mixed, xyb_s, piece)
        arrived(z_back, zb_s, piece)


def on_device(state, gates, wide_gates, angles, coupled, sliced_index, sliced_values):
    rows = state.size // LANES
    linear = state.reshape(2, rows // 2, LANES).transpose(1, 0, 2).reshape(rows, LANES)
    hbm = pl.BlockSpec(memory_space=pltpu.HBM)
    whole = pltpu.VMEM((rows, LANES), F32)
    pieces = pltpu.VMEM((PIECES, rows // PIECES, LANES), F32)
    counts = pltpu.SemaphoreType.DMA((PIECES,))
    result = pl.pallas_call(
        kernel,
        out_shape=pltpu.VMEM((rows, LANES), F32),
        in_specs=[hbm] * 7,
        out_specs=pl.BlockSpec(memory_space=pltpu.VMEM),
        scratch_shapes=[
            pltpu.VMEM(gates.shape, F32),
            pltpu.VMEM(wide_gates.shape, F32),
            pltpu.SMEM(angles.shape, F32),
            pltpu.SMEM(coupled.shape, jnp.int32),
            pltpu.SMEM(sliced_index.shape, jnp.int32),
            pltpu.SMEM(sliced_values.shape, jnp.int32),
            whole, pieces, pieces, pieces, pieces, pieces, pieces, pieces, pieces, pieces, pieces,
            pltpu.VMEM((2, 256, 512), BF16),
            pltpu.VMEM((5, 2, 256, 256), BF16),
            pltpu.VMEM((PIECES, 2, 128, 256), BF16),
            pltpu.SemaphoreType.DMA((4,)),
            pltpu.SemaphoreType.DMA((6,)),
            counts, counts, counts, counts, counts, counts, counts, counts,
        ],
        compiler_params=pltpu.CompilerParams(
            collective_id=0, has_side_effects=True, vmem_limit_bytes=48 << 20
        ),
        cost_estimate=pl.CostEstimate(flops=1 << 31, bytes_accessed=1 << 21, transcendentals=0),
    )(
        *(
            pltpu.with_memory_space_constraint(each, pltpu.HBM)
            for each in (linear, gates, wide_gates, angles, coupled, sliced_index, sliced_values)
        )
    )
    return result.reshape(rows // 2, 2, LANES).transpose(1, 0, 2).reshape(state.shape)


def solution(mesh):
    in_specs = (P(None, ("wide", "narrow")), P(), P(), P(), P(), P(), P())
    out_specs = P(None, ("wide", "narrow"))
    return jax.shard_map(
        on_device, mesh=mesh, in_specs=in_specs, out_specs=out_specs, check_vma=False
    )
```

```python
import functools

import jax
import jax.numpy as jnp
from jax import lax
from jax.experimental import pallas as pl
from jax.experimental.pallas import tpu as pltpu
from jax.sharding import PartitionSpec as P

HIGHEST = lax.Precision.HIGHEST
MESH = pl.DeviceIdType.MESH
PIECES = 4
LANES = 128
F32 = jnp.float32
BF16 = jnp.bfloat16


def iota(shape, axis):
    return lax.broadcasted_iota(jnp.int32, shape, axis)


def split(value):
    high = value.astype(BF16)
    rest = value - high.astype(F32)
    middle = rest.astype(BF16)
    return high, middle, (rest - middle.astype(F32)).astype(BF16)


def thirds(value, axis):
    return jnp.concatenate(split(value), axis=axis)


def dot(left, right):
    return jnp.dot(left, right, preferred_element_type=F32)


def six_products(left, right):
    small = dot(left[0], right[2]) + dot(left[2], right[0]) + dot(left[1], right[1])
    return dot(left[0], right[0]) + (dot(left[0], right[1]) + dot(left[1], right[0]) + small)


def one_hot(wanted, own):
    return jnp.where(wanted == own, 1.0, 0.0).astype(BF16)


def on_lanes(real, imag, taken, given, kept_in, kept_out):
    pair = jnp.concatenate([thirds(real, 0), thirds(imag, 0)], axis=1)
    spread = one_hot(iota((96, 256), 0) % 32, given(iota((96, 256), 1)))
    columns = lax.dot_general(pair, spread, (((0,), (0,)), ((), ())), preferred_element_type=F32)
    to_real = iota((32, 256), 1) % 2 == 0
    from_real, from_imag = columns[:32], columns[32:]
    mixed = jnp.concatenate(
        [jnp.where(to_real, from_real, from_imag), jnp.where(to_real, -from_imag, from_real)], axis=0
    )
    rows = iota((256, 192), 0)
    pick = one_hot(iota((256, 192), 1) % 64, (rows % 2) * 32 + taken(rows))
    full = dot(pick, thirds(mixed, 0))
    return jnp.where(kept_in(iota((256, 256), 0)) == kept_out(iota((256, 256), 1)), full, 0.0)


def middle_index(index):
    return (index // 2) % 32


def middle_kept(index):
    return index // 64


def wide_index(index):
    return (index // 128) * 16 + (index // 2) % 16


def wide_kept(index):
    return (index // 32) % 4


def inner_index(index):
    return ((index // 64) % 2) * 16 + (index // 2) % 16


def inner_kept(index):
    return (index // 128) * 2 + (index // 32) % 2


def kernel(
    state, gates_in, wide_in, angles_in, coupled_in, chosen_in, values_in, out,
    gates, wide, angles, coupled, chosen, values,
    loaded, z_send, z_got, xy_send, xy_got, ready, mixed, late, xy_home, z_back, z_home,
    first_g, rest_g, top_g,
    load_sems, small_sems, z_s, z_r, xy_s, xy_r, xyb_s, xyb_r, zb_s, zb_r,
):
    w = lax.axis_index("wide")
    n = lax.axis_index("narrow")
    x, y, low, core = w // 8, w % 4, (w // 4) % 2, n % 2
    z = (n // 2) * 2 + low
    z_slot = low * 8 + n
    z_name = z * 2 + core
    xy_name = x * 4 + y

    def z_peer(step):
        far = (step - 1) % 8
        other = (z + 4 + (1 - 2 * (far % 2)) * ((far + 1) // 2)) % 8
        side = (core + 1 + (step - 1) // 8) % 2
        lane = (other // 2) * 2 + side
        return (x * 8 + (other % 2) * 4 + y, lane), other * 2 + side, (other % 2) * 8 + lane

    def xy_peer(step):
        across, along = (x + step // 4) % 4, (y + step) % 4
        return (across * 8 + low * 4 + along, n), across * 4 + along

    barrier = pltpu.get_barrier_semaphore()

    loads = [
        pltpu.make_async_copy(
            state.at[pl.ds(part * 512, 512)], loaded.at[pl.ds(part * 512, 512)], load_sems.at[part]
        )
        for part in range(4)
    ]
    for load in loads:
        load.start()

    @pl.loop(1, 16)
    def _(step):
        pl.semaphore_signal(barrier, inc=1, device_id=z_peer(step)[0], device_id_type=MESH)

    @pl.loop(1, 16)
    def _(step):
        pl.semaphore_signal(barrier, inc=1, device_id=xy_peer(step)[0], device_id_type=MESH)

    small = [
        pltpu.make_async_copy(source, target, small_sems.at[place])
        for place, (source, target) in enumerate(
            [
                (gates_in, gates), (wide_in, wide), (angles_in, angles),
                (coupled_in, coupled), (chosen_in, chosen), (values_in, values),
            ]
        )
    ]
    for copy in small:
        copy.start()
    def turn(piece):
        loads[piece].wait()
        for block in range(4):
            start = piece * 512 + block * 128
            turned = loaded[start : start + 128, :].T
            for part in range(8):
                name, half = (block // 2) * 8 + part, (block % 2) * 16
                rows = turned[part * 16 : part * 16 + 16]
                if piece % 2:
                    xy_send[piece, pl.ds(half + name, 16, stride=32), :] = rows
                else:
                    z_send[piece, pl.ds(name * 32 + half, 16), :] = rows

    def slot(index):
        return pl.ds(pl.multiple_of(index * 32, 32), 32)


    def send_z(source, target, sent, got, piece, inward):
        @pl.loop(1, 16)
        def _(step):
            device, name, there = z_peer(step)
            pltpu.make_async_remote_copy(
                src_ref=source.at[piece, slot(name if inward else there)],
                dst_ref=target.at[piece, slot(z_slot if inward else z_name)],
                send_sem=sent.at[piece],
                recv_sem=got.at[piece],
                device_id=device,
                device_id_type=MESH,
            ).start()

        own, landing = (z_name, z_slot) if inward else (z_slot, z_name)
        target[piece, slot(landing), :] = source[piece, slot(own), :]

    def send_xy(source, target, sent, got, piece):
        @pl.loop(1, 16)
        def _(step):
            device, name = xy_peer(step)
            pltpu.make_async_remote_copy(
                src_ref=source.at[piece, slot(name)],
                dst_ref=target.at[piece, slot(xy_name)],
                send_sem=sent.at[piece],
                recv_sem=got.at[piece],
                device_id=device,
                device_id_type=MESH,
            ).start()

        target[piece, slot(xy_name), :] = source[piece, slot(xy_name), :]

    def arrived(buffer, semaphore, piece):
        part = buffer.at[0, pl.ds(0, 480)]
        pltpu.make_async_copy(part, part, semaphore.at[piece]).wait()

    def regroup(source, target, piece):
        for outer in range(16):
            for half in range(2):
                target[piece, pl.ds(outer * 32 + half * 16, 16), :] = source[
                    piece, pl.ds(half * 16 + outer, 16, stride=32), :
                ]

    turn(0)
    pl.semaphore_wait(barrier, 30)
    send_z(z_send, z_got, z_s, z_r, 0, True)
    for piece in range(1, PIECES):
        turn(piece)
    send_xy(xy_send, xy_got, xy_s, xy_r, 1)
    send_z(z_send, z_got, z_s, z_r, 2, True)
    send_xy(xy_send, xy_got, xy_s, xy_r, 3)

    for copy in small:
        copy.wait()
    row, lane = iota((8, 128), 0), iota((8, 128), 1)
    unmixed = (z_name // 8) * 16384 + (z_name % 8) * 16 + xy_name
    place = jnp.where(
        row < 3, (lane % 32) * 128, jnp.where(row < 6, (lane % 4) * 4096, unmixed + (lane % 4) * 32768)
    )
    phases = jnp.zeros((8, 128), F32)
    for layer in range(3):
        for coupling in range(8):
            turn = angles[layer, coupling] * values[chosen[layer, coupling]].astype(F32)
            bit = jnp.right_shift(place, coupled[layer, coupling]) & 1
            counted = jnp.where((row == layer) | (row == layer + 3) | (row == 6), bit, 0)
            phases = phases + turn * counted.astype(F32)
    cosine, sine = jnp.cos(phases), jnp.sin(phases)

    def turned_gate(gate, layer, phase_row):
        real, imag = gate[layer, 0], gate[layer, 1]
        c = cosine[phase_row : phase_row + 1, :32]
        s = sine[phase_row : phase_row + 1, :32]
        return real * c - imag * s, real * s + imag * c

    for layer in range(3):
        real, imag = turned_gate(gates.at[:, 1], layer, layer)
        middle = on_lanes(real, imag, middle_index, middle_index, middle_kept, middle_kept)
        real, imag = wide[layer, 0, 0], wide[layer, 0, 1]
        if layer == 0:
            plain = on_lanes(real, imag, wide_index, inner_index, wide_kept, inner_kept)
            times_i = on_lanes(-imag, real, wide_index, inner_index, wide_kept, inner_kept)
            first = jnp.dot(middle, jnp.concatenate([plain, times_i], axis=1), precision=HIGHEST, preferred_element_type=F32)
            first_g[0], first_g[1], first_g[2] = split(first)
        else:
            plain = on_lanes(real, imag, wide_index, wide_index, wide_kept, wide_kept)
            both = jnp.dot(middle, plain, precision=HIGHEST, preferred_element_type=F32)
            for part, value in enumerate(split(both)):
                rest_g[2 * layer - 1, part] = value
        real, imag = wide[layer, 1, 0], wide[layer, 1, 1]
        if layer < 2:
            second = on_lanes(real, imag, wide_index, wide_index, wide_kept, wide_kept)
        else:
            second = on_lanes(real, imag, inner_index, wide_index, inner_kept, wide_kept)
        for part, value in enumerate(split(second)):
            rest_g[2 * layer, part] = value

    top = [turned_gate(gates.at[:, 0], layer, layer + 3) for layer in range(3)]
    product = jnp.concatenate(top[0], axis=0)
    for real, imag in top[1:]:
        whole = jnp.concatenate(
            [jnp.concatenate([real, -imag], axis=1), jnp.concatenate([imag, real], axis=1)], axis=0
        )
        product = jnp.dot(whole, product, precision=HIGHEST, preferred_element_type=F32)

    def top_index(index):
        return (index % 8) * 4 + ((index // 8) % 2) * 2 + (index // 16) % 2

    def on_rows(real, imag):
        pick = one_hot(iota((128, 96), 1) % 32, top_index(iota((128, 96), 0)))
        part = dot(pick, thirds(jnp.concatenate([real, imag], axis=1), 0))
        columns = iota((192, 256), 1)
        spread = one_hot(iota((192, 256), 0) % 64, ((columns // 32) % 2) * 32 + top_index(columns))
        full = dot(thirds(part, 1), spread)
        return jnp.where(iota((128, 256), 0) // 32 == iota((128, 256), 1) // 64, full, 0.0)

    top_plain = on_rows(product[:32], product[32:])
    top_times_i = on_rows(-product[32:], product[:32])
    for piece in range(PIECES):
        here = (row == 6) & (lane == piece)
        c = jnp.sum(jnp.where(here, cosine, 0.0))
        s = jnp.sum(jnp.where(here, sine, 0.0))
        for part, value in enumerate(split(c * top_plain + s * top_times_i)):
            top_g[piece, part] = value

    def right(tiles, zeros, ones, matrix):
        both = jnp.concatenate(
            [jnp.concatenate([tiles[k] for k in zeros], axis=0), jnp.concatenate([tiles[k] for k in ones], axis=0)], axis=1
        )
        return six_products(split(both), matrix)

    def gates_on(piece):
        tiles = [ready[piece, pl.ds(k * 8, 8), :] for k in range(64)]
        zeros = [k for k in range(64) if not k & 4]
        product = right(tiles, zeros, [k | 4 for k in zeros], [first_g[part] for part in range(3)])
        found = {}
        for place, k in enumerate(zeros):
            for column in range(4):
                found[k, column] = product[place * 8 : place * 8 + 8, column * 128 : column * 128 + 128]
        tiles = [None] * 64
        groups = [k for k in range(64) if not k & 6]
        for start in (0, 8):
            columns = []
            for half in range(2):
                columns.append(
                    jnp.concatenate(
                        [
                            found[k | bit13 * 2, times_i * 2 + bit12]
                            for k in groups[start + 4 * half : start + 4 * half + 4]
                            for times_i in range(2)
                            for bit12 in range(2)
                            for bit13 in range(2)
                        ],
                        axis=0,
                    )
                )
            topped = six_products(
                [top_g[piece, part] for part in range(3)], split(jnp.concatenate(columns, axis=1))
            )
            for half in range(2):
                for which, k in enumerate(groups[start + 4 * half : start + 4 * half + 4]):
                    for bit12 in range(2):
                        for bit13 in range(2):
                            at = which * 32 + bit12 * 16 + bit13 * 8
                            tiles[k | bit12 * 4 | bit13 * 2] = topped[at : at + 8, half * 128 : half * 128 + 128]
        for gate, mask in enumerate((8, 1, 16, 32, 4)):
            zeros = [k for k in range(64) if not k & mask]
            product = right(tiles, zeros, [k | mask for k in zeros], [rest_g[gate, part] for part in range(3)])
            for place, k in enumerate(zeros):
                tiles[k] = product[place * 8 : place * 8 + 8, :128]
                tiles[k | mask] = product[place * 8 : place * 8 + 8, 128:]
        for k in range(64):
            mixed[piece, pl.ds(k * 8, 8), :] = tiles[k]

    @pl.loop(0, PIECES, step=2)
    def _(piece):
        arrived(xy_got, xy_r, piece + 1)
        regroup(xy_got, z_send, piece + 1)
        send_z(z_send, z_got, z_s, z_r, piece + 1, True)
        arrived(z_got, z_r, piece)
        regroup(z_got, xy_send, piece)
        send_xy(xy_send, ready, xy_s, xy_r, piece)

    @pl.loop(0, PIECES)
    def _(piece):
        @pl.when(piece % 2 == 0)
        def _():
            arrived(ready, xy_r, piece)

        @pl.when(piece % 2 == 1)
        def _():
            arrived(z_got, z_r, piece)
            regroup(z_got, ready, piece)

        gates_on(piece)

        @pl.when(piece % 2 == 0)
        def _():
            regroup(mixed, z_back, piece)
            send_z(z_back, z_home, zb_s, zb_r, piece, False)

        @pl.when(piece % 2 == 1)
        def _():
            send_xy(mixed, xy_home, xyb_s, xyb_r, piece)

    @pl.loop(0, PIECES, step=2)
    def _(piece):
        arrived(xy_home, xyb_r, piece + 1)
        regroup(xy_home, z_back, piece + 1)
        send_z(z_back, z_home, zb_s, zb_r, piece + 1, False)
        arrived(z_home, zb_r, piece)
        regroup(z_home, late, piece)
        send_xy(late, xy_home, xyb_s, xyb_r, piece)

    for piece in range(PIECES):
        if piece % 2:
            arrived(z_home, zb_r, piece)
        else:
            arrived(xy_home, xyb_r, piece)
        for block in range(4):
            parts = []
            for part in range(8):
                name, half = (block // 2) * 8 + part, (block % 2) * 16
                if piece % 2:
                    parts.append(z_home[piece, pl.ds(name * 32 + half, 16), :])
                else:
                    parts.append(xy_home[piece, pl.ds(half + name, 16, stride=32), :])
            out[pl.ds(piece * 512 + block * 128, 128), :] = jnp.concatenate(parts, axis=0).T

    for piece in range(PIECES):
        arrived(z_send, z_s, piece)
        arrived(xy_send, xy_s, piece)
        arrived(mixed, xyb_s, piece)
        arrived(z_back, zb_s, piece)


def on_device(state, gates, wide_gates, angles, coupled, sliced_index, sliced_values):
    rows = state.size // LANES
    linear = state.reshape(2, rows // 2, LANES).transpose(1, 0, 2).reshape(rows, LANES)
    hbm = pl.BlockSpec(memory_space=pltpu.HBM)
    whole = pltpu.VMEM((rows, LANES), F32)
    pieces = pltpu.VMEM((PIECES, rows // PIECES, LANES), F32)
    counts = pltpu.SemaphoreType.DMA((PIECES,))
    result = pl.pallas_call(
        kernel,
        out_shape=pltpu.VMEM((rows, LANES), F32),
        in_specs=[hbm] * 7,
        out_specs=pl.BlockSpec(memory_space=pltpu.VMEM),
        scratch_shapes=[
            pltpu.VMEM(gates.shape, F32),
            pltpu.VMEM(wide_gates.shape, F32),
            pltpu.SMEM(angles.shape, F32),
            pltpu.SMEM(coupled.shape, jnp.int32),
            pltpu.SMEM(sliced_index.shape, jnp.int32),
            pltpu.SMEM(sliced_values.shape, jnp.int32),
            whole, pieces, pieces, pieces, pieces, pieces, pieces, pieces, pieces, pieces, pieces,
            pltpu.VMEM((3, 256, 512), BF16),
            pltpu.VMEM((5, 3, 256, 256), BF16),
            pltpu.VMEM((PIECES, 3, 128, 256), BF16),
            pltpu.SemaphoreType.DMA((4,)),
            pltpu.SemaphoreType.DMA((6,)),
            counts, counts, counts, counts, counts, counts, counts, counts,
        ],
        compiler_params=pltpu.CompilerParams(
            collective_id=0, has_side_effects=True, vmem_limit_bytes=48 << 20
        ),
        cost_estimate=pl.CostEstimate(flops=1 << 31, bytes_accessed=1 << 21, transcendentals=0),
    )(
        *(
            pltpu.with_memory_space_constraint(each, pltpu.HBM)
            for each in (linear, gates, wide_gates, angles, coupled, sliced_index, sliced_values)
        )
    )
    return result.reshape(rows // 2, 2, LANES).transpose(1, 0, 2).reshape(state.shape)


def solution(mesh):
    in_specs = (P(None, ("wide", "narrow")), P(), P(), P(), P(), P(), P())
    out_specs = P(None, ("wide", "narrow"))
    return jax.shard_map(
        on_device, mesh=mesh, in_specs=in_specs, out_specs=out_specs, check_vma=False
    )
```

```python
import functools

import jax
import jax.numpy as jnp
from jax import lax
from jax.experimental import pallas as pl
from jax.experimental.pallas import tpu as pltpu
from jax.sharding import PartitionSpec as P

HIGHEST = lax.Precision.HIGHEST
MESH = pl.DeviceIdType.MESH
PIECES = 4
LANES = 128
F32 = jnp.float32
BF16 = jnp.bfloat16


def iota(shape, axis):
    return lax.broadcasted_iota(jnp.int32, shape, axis)


def split(value):
    high = value.astype(BF16)
    rest = value - high.astype(F32)
    middle = rest.astype(BF16)
    return high, middle, (rest - middle.astype(F32)).astype(BF16)


def thirds(value, axis):
    return jnp.concatenate(split(value), axis=axis)


def dot(left, right):
    return jnp.dot(left, right, preferred_element_type=F32)


def six_products(left, right):
    small = dot(left[0], right[2]) + dot(left[2], right[0]) + dot(left[1], right[1])
    return dot(left[0], right[0]) + (dot(left[0], right[1]) + dot(left[1], right[0]) + small)


def one_hot(wanted, own):
    return jnp.where(wanted == own, 1.0, 0.0).astype(BF16)


def on_lanes(real, imag, taken, given, kept_in, kept_out):
    pair = jnp.concatenate([thirds(real, 0), thirds(imag, 0)], axis=1)
    spread = one_hot(iota((96, 256), 0) % 32, given(iota((96, 256), 1)))
    columns = lax.dot_general(pair, spread, (((0,), (0,)), ((), ())), preferred_element_type=F32)
    to_real = iota((32, 256), 1) % 2 == 0
    from_real, from_imag = columns[:32], columns[32:]
    mixed = jnp.concatenate(
        [jnp.where(to_real, from_real, from_imag), jnp.where(to_real, -from_imag, from_real)], axis=0
    )
    rows = iota((256, 192), 0)
    pick = one_hot(iota((256, 192), 1) % 64, (rows % 2) * 32 + taken(rows))
    full = dot(pick, thirds(mixed, 0))
    return jnp.where(kept_in(iota((256, 256), 0)) == kept_out(iota((256, 256), 1)), full, 0.0)


def middle_index(index):
    return (index // 2) % 32


def middle_kept(index):
    return index // 64


def wide_index(index):
    return (index // 128) * 16 + (index // 2) % 16


def wide_kept(index):
    return (index // 32) % 4


def inner_index(index):
    return ((index // 64) % 2) * 16 + (index // 2) % 16


def inner_kept(index):
    return (index // 128) * 2 + (index // 32) % 2


def kernel(
    state, gates_in, wide_in, angles_in, coupled_in, chosen_in, values_in, out,
    gates, wide, angles, coupled, chosen, values,
    loaded, z_send, z_got, xy_send, xy_got, ready, mixed, late, xy_home, z_back, z_home,
    first_g, rest_g, top_g,
    load_sems, small_sems, z_s, z_r, xy_s, xy_r, xyb_s, xyb_r, zb_s, zb_r,
):
    w = lax.axis_index("wide")
    n = lax.axis_index("narrow")
    x, y, low, core = w // 8, w % 4, (w // 4) % 2, n % 2
    z = (n // 2) * 2 + low
    z_slot = low * 8 + n
    z_name = z * 2 + core
    xy_name = x * 4 + y

    def z_peer(step):
        far = (step - 1) % 8
        other = lax.rem(z + (4 + (1 - 2 * (far % 2)) * ((far + 1) // 2)), 8)
        side = lax.rem(core + (1 + (step - 1) // 8), 2)
        lane = (other // 2) * 2 + side
        return (x * 8 + lax.rem(other, 2) * 4 + y, lane), other * 2 + side, lax.rem(other, 2) * 8 + lane

    def xy_peer(step):
        across, along = lax.rem(x + step // 4, 4), lax.rem(y + step % 4, 4)
        return (across * 8 + low * 4 + along, n), across * 4 + along

    barrier = pltpu.get_barrier_semaphore()

    loads = [
        pltpu.make_async_copy(
            state.at[pl.ds(part * 512, 512)], loaded.at[pl.ds(part * 512, 512)], load_sems.at[part]
        )
        for part in range(4)
    ]
    for load in loads:
        load.start()

    for step in range(1, 16):
        pl.semaphore_signal(barrier, inc=1, device_id=z_peer(step)[0], device_id_type=MESH)
    for step in range(1, 16):
        pl.semaphore_signal(barrier, inc=1, device_id=xy_peer(step)[0], device_id_type=MESH)

    small = [
        pltpu.make_async_copy(source, target, small_sems.at[place])
        for place, (source, target) in enumerate(
            [
                (gates_in, gates), (wide_in, wide), (angles_in, angles),
                (coupled_in, coupled), (chosen_in, chosen), (values_in, values),
            ]
        )
    ]
    for copy in small:
        copy.start()
    def turn(piece):
        loads[piece].wait()
        for block in range(4):
            start = piece * 512 + block * 128
            turned = loaded[start : start + 128, :].T
            for part in range(8):
                name, half = (block // 2) * 8 + part, (block % 2) * 16
                rows = turned[part * 16 : part * 16 + 16]
                if piece % 2:
                    xy_send[piece, pl.ds(half + name, 16, stride=32), :] = rows
                else:
                    z_send[piece, pl.ds(name * 32 + half, 16), :] = rows

    def slot(index):
        return pl.ds(pl.multiple_of(index * 32, 32), 32)


    def send_z(source, target, sent, got, piece, inward):
        @pl.loop(1, 16)
        def _(step):
            device, name, there = z_peer(step)
            pltpu.make_async_remote_copy(
                src_ref=source.at[piece, slot(name if inward else there)],
                dst_ref=target.at[piece, slot(z_slot if inward else z_name)],
                send_sem=sent.at[piece],
                recv_sem=got.at[piece],
                device_id=device,
                device_id_type=MESH,
            ).start()

        own, landing = (z_name, z_slot) if inward else (z_slot, z_name)
        target[piece, slot(landing), :] = source[piece, slot(own), :]

    def send_xy(source, target, sent, got, piece):
        @pl.loop(1, 16)
        def _(step):
            device, name = xy_peer(step)
            pltpu.make_async_remote_copy(
                src_ref=source.at[piece, slot(name)],
                dst_ref=target.at[piece, slot(xy_name)],
                send_sem=sent.at[piece],
                recv_sem=got.at[piece],
                device_id=device,
                device_id_type=MESH,
            ).start()

        target[piece, slot(xy_name), :] = source[piece, slot(xy_name), :]

    def arrived(buffer, semaphore, piece):
        part = buffer.at[0, pl.ds(0, 480)]
        pltpu.make_async_copy(part, part, semaphore.at[piece]).wait()

    def regroup(source, target, piece):
        for outer in range(16):
            for half in range(2):
                target[piece, pl.ds(outer * 32 + half * 16, 16), :] = source[
                    piece, pl.ds(half * 16 + outer, 16, stride=32), :
                ]

    turn(0)
    pl.semaphore_wait(barrier, 30)
    send_z(z_send, z_got, z_s, z_r, 0, True)
    for piece in range(1, PIECES):
        turn(piece)
    send_xy(xy_send, xy_got, xy_s, xy_r, 1)
    send_z(z_send, z_got, z_s, z_r, 2, True)
    send_xy(xy_send, xy_got, xy_s, xy_r, 3)

    for copy in small:
        copy.wait()
    row, lane = iota((8, 128), 0), iota((8, 128), 1)
    unmixed = (z_name // 8) * 16384 + (z_name % 8) * 16 + xy_name
    place = jnp.where(
        row < 3, (lane % 32) * 128, jnp.where(row < 6, (lane % 4) * 4096, unmixed + (lane % 4) * 32768)
    )
    phases = jnp.zeros((8, 128), F32)
    for layer in range(3):
        for coupling in range(8):
            turn = angles[layer, coupling] * values[chosen[layer, coupling]].astype(F32)
            bit = jnp.right_shift(place, coupled[layer, coupling]) & 1
            counted = jnp.where((row == layer) | (row == layer + 3) | (row == 6), bit, 0)
            phases = phases + turn * counted.astype(F32)
    cosine, sine = jnp.cos(phases), jnp.sin(phases)

    def turned_gate(gate, layer, phase_row):
        real, imag = gate[layer, 0], gate[layer, 1]
        c = cosine[phase_row : phase_row + 1, :32]
        s = sine[phase_row : phase_row + 1, :32]
        return real * c - imag * s, real * s + imag * c

    for layer in range(3):
        real, imag = turned_gate(gates.at[:, 1], layer, layer)
        middle = on_lanes(real, imag, middle_index, middle_index, middle_kept, middle_kept)
        real, imag = wide[layer, 0, 0], wide[layer, 0, 1]
        if layer == 0:
            plain = on_lanes(real, imag, wide_index, inner_index, wide_kept, inner_kept)
            times_i = on_lanes(-imag, real, wide_index, inner_index, wide_kept, inner_kept)
            first = jnp.dot(middle, jnp.concatenate([plain, times_i], axis=1), precision=HIGHEST, preferred_element_type=F32)
            first_g[0], first_g[1], first_g[2] = split(first)
        else:
            plain = on_lanes(real, imag, wide_index, wide_index, wide_kept, wide_kept)
            both = jnp.dot(middle, plain, precision=HIGHEST, preferred_element_type=F32)
            for part, value in enumerate(split(both)):
                rest_g[2 * layer - 1, part] = value
        real, imag = wide[layer, 1, 0], wide[layer, 1, 1]
        if layer < 2:
            second = on_lanes(real, imag, wide_index, wide_index, wide_kept, wide_kept)
        else:
            second = on_lanes(real, imag, inner_index, wide_index, inner_kept, wide_kept)
        for part, value in enumerate(split(second)):
            rest_g[2 * layer, part] = value

    top = [turned_gate(gates.at[:, 0], layer, layer + 3) for layer in range(3)]
    product = jnp.concatenate(top[0], axis=0)
    for real, imag in top[1:]:
        whole = jnp.concatenate(
            [jnp.concatenate([real, -imag], axis=1), jnp.concatenate([imag, real], axis=1)], axis=0
        )
        product = jnp.dot(whole, product, precision=HIGHEST, preferred_element_type=F32)

    def top_index(index):
        return (index % 8) * 4 + ((index // 8) % 2) * 2 + (index // 16) % 2

    def on_rows(real, imag):
        pick = one_hot(iota((128, 96), 1) % 32, top_index(iota((128, 96), 0)))
        part = dot(pick, thirds(jnp.concatenate([real, imag], axis=1), 0))
        columns = iota((192, 256), 1)
        spread = one_hot(iota((192, 256), 0) % 64, ((columns // 32) % 2) * 32 + top_index(columns))
        full = dot(thirds(part, 1), spread)
        return jnp.where(iota((128, 256), 0) // 32 == iota((128, 256), 1) // 64, full, 0.0)

    top_plain = on_rows(product[:32], product[32:])
    top_times_i = on_rows(-product[32:], product[:32])
    for piece in range(PIECES):
        here = (row == 6) & (lane == piece)
        c = jnp.sum(jnp.where(here, cosine, 0.0))
        s = jnp.sum(jnp.where(here, sine, 0.0))
        for part, value in enumerate(split(c * top_plain + s * top_times_i)):
            top_g[piece, part] = value

    def right(tiles, zeros, ones, matrix):
        both = jnp.concatenate(
            [jnp.concatenate([tiles[k] for k in zeros], axis=0), jnp.concatenate([tiles[k] for k in ones], axis=0)], axis=1
        )
        return six_products(split(both), matrix)

    def gates_on(piece):
        tiles = [ready[piece, pl.ds(k * 8, 8), :] for k in range(64)]
        zeros = [k for k in range(64) if not k & 4]
        product = right(tiles, zeros, [k | 4 for k in zeros], [first_g[part] for part in range(3)])
        found = {}
        for place, k in enumerate(zeros):
            for column in range(4):
                found[k, column] = product[place * 8 : place * 8 + 8, column * 128 : column * 128 + 128]
        tiles = [None] * 64
        groups = [k for k in range(64) if not k & 6]
        for start in (0, 8):
            columns = []
            for half in range(2):
                columns.append(
                    jnp.concatenate(
                        [
                            found[k | bit13 * 2, times_i * 2 + bit12]
                            for k in groups[start + 4 * half : start + 4 * half + 4]
                            for times_i in range(2)
                            for bit12 in range(2)
                            for bit13 in range(2)
                        ],
                        axis=0,
                    )
                )
            topped = six_products(
                [top_g[piece, part] for part in range(3)], split(jnp.concatenate(columns, axis=1))
            )
            for half in range(2):
                for which, k in enumerate(groups[start + 4 * half : start + 4 * half + 4]):
                    for bit12 in range(2):
                        for bit13 in range(2):
                            at = which * 32 + bit12 * 16 + bit13 * 8
                            tiles[k | bit12 * 4 | bit13 * 2] = topped[at : at + 8, half * 128 : half * 128 + 128]
        for gate, mask in enumerate((8, 1, 16, 32, 4)):
            zeros = [k for k in range(64) if not k & mask]
            product = right(tiles, zeros, [k | mask for k in zeros], [rest_g[gate, part] for part in range(3)])
            for place, k in enumerate(zeros):
                tiles[k] = product[place * 8 : place * 8 + 8, :128]
                tiles[k | mask] = product[place * 8 : place * 8 + 8, 128:]
        for k in range(64):
            mixed[piece, pl.ds(k * 8, 8), :] = tiles[k]

    @pl.loop(0, PIECES, step=2)
    def _(piece):
        arrived(xy_got, xy_r, piece + 1)
        regroup(xy_got, z_send, piece + 1)
        send_z(z_send, z_got, z_s, z_r, piece + 1, True)
        arrived(z_got, z_r, piece)
        regroup(z_got, xy_send, piece)
        send_xy(xy_send, ready, xy_s, xy_r, piece)

    @pl.loop(0, PIECES)
    def _(piece):
        @pl.when(piece % 2 == 0)
        def _():
            arrived(ready, xy_r, piece)

        @pl.when(piece % 2 == 1)
        def _():
            arrived(z_got, z_r, piece)
            regroup(z_got, ready, piece)

        gates_on(piece)

        @pl.when(piece % 2 == 0)
        def _():
            regroup(mixed, z_back, piece)
            send_z(z_back, z_home, zb_s, zb_r, piece, False)

        @pl.when(piece % 2 == 1)
        def _():
            send_xy(mixed, xy_home, xyb_s, xyb_r, piece)

    @pl.loop(0, PIECES, step=2)
    def _(piece):
        arrived(xy_home, xyb_r, piece + 1)
        regroup(xy_home, z_back, piece + 1)
        send_z(z_back, z_home, zb_s, zb_r, piece + 1, False)
        arrived(z_home, zb_r, piece)
        regroup(z_home, late, piece)
        send_xy(late, xy_home, xyb_s, xyb_r, piece)

    for piece in range(PIECES):
        if piece % 2:
            arrived(z_home, zb_r, piece)
        else:
            arrived(xy_home, xyb_r, piece)
        for block in range(4):
            parts = []
            for part in range(8):
                name, half = (block // 2) * 8 + part, (block % 2) * 16
                if piece % 2:
                    parts.append(z_home[piece, pl.ds(name * 32 + half, 16), :])
                else:
                    parts.append(xy_home[piece, pl.ds(half + name, 16, stride=32), :])
            out[pl.ds(piece * 512 + block * 128, 128), :] = jnp.concatenate(parts, axis=0).T

    for piece in range(PIECES):
        arrived(z_send, z_s, piece)
        arrived(xy_send, xy_s, piece)
        arrived(mixed, xyb_s, piece)
        arrived(z_back, zb_s, piece)


def on_device(state, gates, wide_gates, angles, coupled, sliced_index, sliced_values):
    rows = state.size // LANES
    linear = state.reshape(2, rows // 2, LANES).transpose(1, 0, 2).reshape(rows, LANES)
    hbm = pl.BlockSpec(memory_space=pltpu.HBM)
    whole = pltpu.VMEM((rows, LANES), F32)
    pieces = pltpu.VMEM((PIECES, rows // PIECES, LANES), F32)
    counts = pltpu.SemaphoreType.DMA((PIECES,))
    result = pl.pallas_call(
        kernel,
        out_shape=pltpu.VMEM((rows, LANES), F32),
        in_specs=[hbm] * 7,
        out_specs=pl.BlockSpec(memory_space=pltpu.VMEM),
        scratch_shapes=[
            pltpu.VMEM(gates.shape, F32),
            pltpu.VMEM(wide_gates.shape, F32),
            pltpu.SMEM(angles.shape, F32),
            pltpu.SMEM(coupled.shape, jnp.int32),
            pltpu.SMEM(sliced_index.shape, jnp.int32),
            pltpu.SMEM(sliced_values.shape, jnp.int32),
            whole, pieces, pieces, pieces, pieces, pieces, pieces, pieces, pieces, pieces, pieces,
            pltpu.VMEM((3, 256, 512), BF16),
            pltpu.VMEM((5, 3, 256, 256), BF16),
            pltpu.VMEM((PIECES, 3, 128, 256), BF16),
            pltpu.SemaphoreType.DMA((4,)),
            pltpu.SemaphoreType.DMA((6,)),
            counts, counts, counts, counts, counts, counts, counts, counts,
        ],
        compiler_params=pltpu.CompilerParams(
            collective_id=0, has_side_effects=True, vmem_limit_bytes=48 << 20
        ),
        cost_estimate=pl.CostEstimate(flops=1 << 31, bytes_accessed=1 << 21, transcendentals=0),
    )(
        *(
            pltpu.with_memory_space_constraint(each, pltpu.HBM)
            for each in (linear, gates, wide_gates, angles, coupled, sliced_index, sliced_values)
        )
    )
    return result.reshape(rows // 2, 2, LANES).transpose(1, 0, 2).reshape(state.shape)


def solution(mesh):
    in_specs = (P(None, ("wide", "narrow")), P(), P(), P(), P(), P(), P())
    out_specs = P(None, ("wide", "narrow"))
    return jax.shard_map(
        on_device, mesh=mesh, in_specs=in_specs, out_specs=out_specs, check_vma=False
    )
```

```python
import functools

import jax
import jax.numpy as jnp
from jax import lax
from jax.experimental import pallas as pl
from jax.experimental.pallas import tpu as pltpu
from jax.sharding import PartitionSpec as P

HIGHEST = lax.Precision.HIGHEST
MESH = pl.DeviceIdType.MESH
PIECES = 4
LANES = 128
F32 = jnp.float32
BF16 = jnp.bfloat16


def iota(shape, axis):
    return lax.broadcasted_iota(jnp.int32, shape, axis)


def split(value):
    high = value.astype(BF16)
    rest = value - high.astype(F32)
    middle = rest.astype(BF16)
    return high, middle, (rest - middle.astype(F32)).astype(BF16)


def thirds(value, axis):
    return jnp.concatenate(split(value), axis=axis)


def dot(left, right):
    return jnp.dot(left, right, preferred_element_type=F32)


def six_products(left, right):
    small = dot(left[0], right[2]) + dot(left[2], right[0]) + dot(left[1], right[1])
    return dot(left[0], right[0]) + (dot(left[0], right[1]) + dot(left[1], right[0]) + small)


def one_hot(wanted, own):
    return jnp.where(wanted == own, 1.0, 0.0).astype(BF16)


def on_lanes(real, imag, taken, given, kept_in, kept_out):
    pair = jnp.concatenate([thirds(real, 0), thirds(imag, 0)], axis=1)
    spread = one_hot(iota((96, 256), 0) % 32, given(iota((96, 256), 1)))
    columns = lax.dot_general(pair, spread, (((0,), (0,)), ((), ())), preferred_element_type=F32)
    to_real = iota((32, 256), 1) % 2 == 0
    from_real, from_imag = columns[:32], columns[32:]
    mixed = jnp.concatenate(
        [jnp.where(to_real, from_real, from_imag), jnp.where(to_real, -from_imag, from_real)], axis=0
    )
    rows = iota((256, 192), 0)
    pick = one_hot(iota((256, 192), 1) % 64, (rows % 2) * 32 + taken(rows))
    full = dot(pick, thirds(mixed, 0))
    return jnp.where(kept_in(iota((256, 256), 0)) == kept_out(iota((256, 256), 1)), full, 0.0)


def middle_index(index):
    return (index // 2) % 32


def middle_kept(index):
    return index // 64


def wide_index(index):
    return (index // 128) * 16 + (index // 2) % 16


def wide_kept(index):
    return (index // 32) % 4


def inner_index(index):
    return ((index // 64) % 2) * 16 + (index // 2) % 16


def inner_kept(index):
    return (index // 128) * 2 + (index // 32) % 2


def kernel(
    state, gates_in, wide_in, angles_in, coupled_in, chosen_in, values_in, out,
    gates, wide, angles, coupled, chosen, values,
    loaded, z_send, z_got, xy_send, xy_got, ready, mixed, late, xy_home, z_back, z_home,
    first_g, rest_g, top_g,
    load_sems, small_sems, z_s, z_r, xy_s, xy_r, xyb_s, xyb_r, zb_s, zb_r,
):
    w = lax.axis_index("wide")
    n = lax.axis_index("narrow")
    x, y, low, core = w // 8, w % 4, (w // 4) % 2, n % 2
    z = (n // 2) * 2 + low
    z_slot = low * 8 + n
    z_name = z * 2 + core
    xy_name = x * 4 + y

    def z_peer(step):
        far = (step - 1) % 8
        other = lax.rem(z + (4 + (1 - 2 * (far % 2)) * ((far + 1) // 2)), 8)
        side = lax.rem(core + (1 + (step - 1) // 8), 2)
        lane = (other // 2) * 2 + side
        return (x * 8 + lax.rem(other, 2) * 4 + y, lane), other * 2 + side, lax.rem(other, 2) * 8 + lane

    def xy_peer(step):
        across, along = lax.rem(x + step // 4, 4), lax.rem(y + step % 4, 4)
        return (across * 8 + low * 4 + along, n), across * 4 + along

    barrier = pltpu.get_barrier_semaphore()

    loads = [
        pltpu.make_async_copy(
            state.at[pl.ds(part * 512, 512)], loaded.at[pl.ds(part * 512, 512)], load_sems.at[part]
        )
        for part in range(4)
    ]
    for load in loads:
        load.start()

    for step in range(1, 16):
        pl.semaphore_signal(barrier, inc=1, device_id=z_peer(step)[0], device_id_type=MESH)
    for step in range(1, 16):
        pl.semaphore_signal(barrier, inc=1, device_id=xy_peer(step)[0], device_id_type=MESH)

    small = [
        pltpu.make_async_copy(source, target, small_sems.at[place])
        for place, (source, target) in enumerate(
            [
                (gates_in, gates), (wide_in, wide), (angles_in, angles),
                (coupled_in, coupled), (chosen_in, chosen), (values_in, values),
            ]
        )
    ]
    for copy in small:
        copy.start()
    def turn(piece):
        loads[piece].wait()
        for block in range(4):
            start = piece * 512 + block * 128
            turned = loaded[start : start + 128, :].T
            for part in range(8):
                name, half = (block // 2) * 8 + part, (block % 2) * 16
                rows = turned[part * 16 : part * 16 + 16]
                if piece % 2:
                    xy_send[piece, pl.ds(half + name, 16, stride=32), :] = rows
                else:
                    z_send[piece, pl.ds(name * 32 + half, 16), :] = rows

    def slot(index):
        return pl.ds(pl.multiple_of(index * 32, 32), 32)


    def send_z(source, target, sent, got, piece, inward):
        for step in range(1, 16):
            device, name, there = z_peer(step)
            pltpu.make_async_remote_copy(
                src_ref=source.at[piece, slot(name if inward else there)],
                dst_ref=target.at[piece, slot(z_slot if inward else z_name)],
                send_sem=sent.at[piece],
                recv_sem=got.at[piece],
                device_id=device,
                device_id_type=MESH,
            ).start()

        own, landing = (z_name, z_slot) if inward else (z_slot, z_name)
        target[piece, slot(landing), :] = source[piece, slot(own), :]

    def send_xy(source, target, sent, got, piece):
        for step in range(1, 16):
            device, name = xy_peer(step)
            pltpu.make_async_remote_copy(
                src_ref=source.at[piece, slot(name)],
                dst_ref=target.at[piece, slot(xy_name)],
                send_sem=sent.at[piece],
                recv_sem=got.at[piece],
                device_id=device,
                device_id_type=MESH,
            ).start()

        target[piece, slot(xy_name), :] = source[piece, slot(xy_name), :]

    def arrived(buffer, semaphore, piece):
        part = buffer.at[0, pl.ds(0, 480)]
        pltpu.make_async_copy(part, part, semaphore.at[piece]).wait()

    def regroup(source, target, piece):
        for outer in range(16):
            for half in range(2):
                target[piece, pl.ds(outer * 32 + half * 16, 16), :] = source[
                    piece, pl.ds(half * 16 + outer, 16, stride=32), :
                ]

    turn(0)
    pl.semaphore_wait(barrier, 30)
    send_z(z_send, z_got, z_s, z_r, 0, True)
    for piece in range(1, PIECES):
        turn(piece)
    send_xy(xy_send, xy_got, xy_s, xy_r, 1)
    send_z(z_send, z_got, z_s, z_r, 2, True)
    send_xy(xy_send, xy_got, xy_s, xy_r, 3)

    for copy in small:
        copy.wait()
    row, lane = iota((8, 128), 0), iota((8, 128), 1)
    unmixed = (z_name // 8) * 16384 + (z_name % 8) * 16 + xy_name
    place = jnp.where(
        row < 3, (lane % 32) * 128, jnp.where(row < 6, (lane % 4) * 4096, unmixed + (lane % 4) * 32768)
    )
    phases = jnp.zeros((8, 128), F32)
    for layer in range(3):
        for coupling in range(8):
            turn = angles[layer, coupling] * values[chosen[layer, coupling]].astype(F32)
            bit = jnp.right_shift(place, coupled[layer, coupling]) & 1
            counted = jnp.where((row == layer) | (row == layer + 3) | (row == 6), bit, 0)
            phases = phases + turn * counted.astype(F32)
    cosine, sine = jnp.cos(phases), jnp.sin(phases)

    def turned_gate(gate, layer, phase_row):
        real, imag = gate[layer, 0], gate[layer, 1]
        c = cosine[phase_row : phase_row + 1, :32]
        s = sine[phase_row : phase_row + 1, :32]
        return real * c - imag * s, real * s + imag * c

    for layer in range(3):
        real, imag = turned_gate(gates.at[:, 1], layer, layer)
        middle = on_lanes(real, imag, middle_index, middle_index, middle_kept, middle_kept)
        real, imag = wide[layer, 0, 0], wide[layer, 0, 1]
        if layer == 0:
            plain = on_lanes(real, imag, wide_index, inner_index, wide_kept, inner_kept)
            times_i = on_lanes(-imag, real, wide_index, inner_index, wide_kept, inner_kept)
            first = jnp.dot(middle, jnp.concatenate([plain, times_i], axis=1), precision=HIGHEST, preferred_element_type=F32)
            first_g[0], first_g[1], first_g[2] = split(first)
        else:
            plain = on_lanes(real, imag, wide_index, wide_index, wide_kept, wide_kept)
            both = jnp.dot(middle, plain, precision=HIGHEST, preferred_element_type=F32)
            for part, value in enumerate(split(both)):
                rest_g[2 * layer - 1, part] = value
        real, imag = wide[layer, 1, 0], wide[layer, 1, 1]
        if layer < 2:
            second = on_lanes(real, imag, wide_index, wide_index, wide_kept, wide_kept)
        else:
            second = on_lanes(real, imag, inner_index, wide_index, inner_kept, wide_kept)
        for part, value in enumerate(split(second)):
            rest_g[2 * layer, part] = value

    top = [turned_gate(gates.at[:, 0], layer, layer + 3) for layer in range(3)]
    product = jnp.concatenate(top[0], axis=0)
    for real, imag in top[1:]:
        whole = jnp.concatenate(
            [jnp.concatenate([real, -imag], axis=1), jnp.concatenate([imag, real], axis=1)], axis=0
        )
        product = jnp.dot(whole, product, precision=HIGHEST, preferred_element_type=F32)

    def top_index(index):
        return (index % 8) * 4 + ((index // 8) % 2) * 2 + (index // 16) % 2

    def on_rows(real, imag):
        pick = one_hot(iota((128, 96), 1) % 32, top_index(iota((128, 96), 0)))
        part = dot(pick, thirds(jnp.concatenate([real, imag], axis=1), 0))
        columns = iota((192, 256), 1)
        spread = one_hot(iota((192, 256), 0) % 64, ((columns // 32) % 2) * 32 + top_index(columns))
        full = dot(thirds(part, 1), spread)
        return jnp.where(iota((128, 256), 0) // 32 == iota((128, 256), 1) // 64, full, 0.0)

    top_plain = on_rows(product[:32], product[32:])
    top_times_i = on_rows(-product[32:], product[:32])
    for piece in range(PIECES):
        here = (row == 6) & (lane == piece)
        c = jnp.sum(jnp.where(here, cosine, 0.0))
        s = jnp.sum(jnp.where(here, sine, 0.0))
        for part, value in enumerate(split(c * top_plain + s * top_times_i)):
            top_g[piece, part] = value

    def right(tiles, zeros, ones, matrix):
        both = jnp.concatenate(
            [jnp.concatenate([tiles[k] for k in zeros], axis=0), jnp.concatenate([tiles[k] for k in ones], axis=0)], axis=1
        )
        return six_products(split(both), matrix)

    def gates_on(piece):
        tiles = [ready[piece, pl.ds(k * 8, 8), :] for k in range(64)]
        zeros = [k for k in range(64) if not k & 4]
        product = right(tiles, zeros, [k | 4 for k in zeros], [first_g[part] for part in range(3)])
        found = {}
        for place, k in enumerate(zeros):
            for column in range(4):
                found[k, column] = product[place * 8 : place * 8 + 8, column * 128 : column * 128 + 128]
        tiles = [None] * 64
        groups = [k for k in range(64) if not k & 6]
        for start in (0, 8):
            columns = []
            for half in range(2):
                columns.append(
                    jnp.concatenate(
                        [
                            found[k | bit13 * 2, times_i * 2 + bit12]
                            for k in groups[start + 4 * half : start + 4 * half + 4]
                            for times_i in range(2)
                            for bit12 in range(2)
                            for bit13 in range(2)
                        ],
                        axis=0,
                    )
                )
            topped = six_products(
                [top_g[piece, part] for part in range(3)], split(jnp.concatenate(columns, axis=1))
            )
            for half in range(2):
                for which, k in enumerate(groups[start + 4 * half : start + 4 * half + 4]):
                    for bit12 in range(2):
                        for bit13 in range(2):
                            at = which * 32 + bit12 * 16 + bit13 * 8
                            tiles[k | bit12 * 4 | bit13 * 2] = topped[at : at + 8, half * 128 : half * 128 + 128]
        for gate, mask in enumerate((8, 1, 16, 32, 4)):
            zeros = [k for k in range(64) if not k & mask]
            product = right(tiles, zeros, [k | mask for k in zeros], [rest_g[gate, part] for part in range(3)])
            for place, k in enumerate(zeros):
                tiles[k] = product[place * 8 : place * 8 + 8, :128]
                tiles[k | mask] = product[place * 8 : place * 8 + 8, 128:]
        for k in range(64):
            mixed[piece, pl.ds(k * 8, 8), :] = tiles[k]

    @pl.loop(0, PIECES, step=2)
    def _(piece):
        arrived(xy_got, xy_r, piece + 1)
        regroup(xy_got, z_send, piece + 1)
        send_z(z_send, z_got, z_s, z_r, piece + 1, True)
        arrived(z_got, z_r, piece)
        regroup(z_got, xy_send, piece)
        send_xy(xy_send, ready, xy_s, xy_r, piece)

    @pl.loop(0, PIECES)
    def _(piece):
        @pl.when(piece % 2 == 0)
        def _():
            arrived(ready, xy_r, piece)

        @pl.when(piece % 2 == 1)
        def _():
            arrived(z_got, z_r, piece)
            regroup(z_got, ready, piece)

        gates_on(piece)

        @pl.when(piece % 2 == 0)
        def _():
            regroup(mixed, z_back, piece)
            send_z(z_back, z_home, zb_s, zb_r, piece, False)

        @pl.when(piece % 2 == 1)
        def _():
            send_xy(mixed, xy_home, xyb_s, xyb_r, piece)

    @pl.loop(0, PIECES, step=2)
    def _(piece):
        arrived(xy_home, xyb_r, piece + 1)
        regroup(xy_home, z_back, piece + 1)
        send_z(z_back, z_home, zb_s, zb_r, piece + 1, False)
        arrived(z_home, zb_r, piece)
        regroup(z_home, late, piece)
        send_xy(late, xy_home, xyb_s, xyb_r, piece)

    for piece in range(PIECES):
        if piece % 2:
            arrived(z_home, zb_r, piece)
        else:
            arrived(xy_home, xyb_r, piece)
        for block in range(4):
            parts = []
            for part in range(8):
                name, half = (block // 2) * 8 + part, (block % 2) * 16
                if piece % 2:
                    parts.append(z_home[piece, pl.ds(name * 32 + half, 16), :])
                else:
                    parts.append(xy_home[piece, pl.ds(half + name, 16, stride=32), :])
            out[pl.ds(piece * 512 + block * 128, 128), :] = jnp.concatenate(parts, axis=0).T

    for piece in range(PIECES):
        arrived(z_send, z_s, piece)
        arrived(xy_send, xy_s, piece)
        arrived(mixed, xyb_s, piece)
        arrived(z_back, zb_s, piece)


def on_device(state, gates, wide_gates, angles, coupled, sliced_index, sliced_values):
    rows = state.size // LANES
    linear = state.reshape(2, rows // 2, LANES).transpose(1, 0, 2).reshape(rows, LANES)
    hbm = pl.BlockSpec(memory_space=pltpu.HBM)
    whole = pltpu.VMEM((rows, LANES), F32)
    pieces = pltpu.VMEM((PIECES, rows // PIECES, LANES), F32)
    counts = pltpu.SemaphoreType.DMA((PIECES,))
    result = pl.pallas_call(
        kernel,
        out_shape=pltpu.VMEM((rows, LANES), F32),
        in_specs=[hbm] * 7,
        out_specs=pl.BlockSpec(memory_space=pltpu.VMEM),
        scratch_shapes=[
            pltpu.VMEM(gates.shape, F32),
            pltpu.VMEM(wide_gates.shape, F32),
            pltpu.SMEM(angles.shape, F32),
            pltpu.SMEM(coupled.shape, jnp.int32),
            pltpu.SMEM(sliced_index.shape, jnp.int32),
            pltpu.SMEM(sliced_values.shape, jnp.int32),
            whole, pieces, pieces, pieces, pieces, pieces, pieces, pieces, pieces, pieces, pieces,
            pltpu.VMEM((3, 256, 512), BF16),
            pltpu.VMEM((5, 3, 256, 256), BF16),
            pltpu.VMEM((PIECES, 3, 128, 256), BF16),
            pltpu.SemaphoreType.DMA((4,)),
            pltpu.SemaphoreType.DMA((6,)),
            counts, counts, counts, counts, counts, counts, counts, counts,
        ],
        compiler_params=pltpu.CompilerParams(
            collective_id=0, has_side_effects=True, vmem_limit_bytes=48 << 20
        ),
        cost_estimate=pl.CostEstimate(flops=1 << 31, bytes_accessed=1 << 21, transcendentals=0),
    )(
        *(
            pltpu.with_memory_space_constraint(each, pltpu.HBM)
            for each in (linear, gates, wide_gates, angles, coupled, sliced_index, sliced_values)
        )
    )
    return result.reshape(rows // 2, 2, LANES).transpose(1, 0, 2).reshape(state.shape)


def solution(mesh):
    in_specs = (P(None, ("wide", "narrow")), P(), P(), P(), P(), P(), P())
    out_specs = P(None, ("wide", "narrow"))
    return jax.shard_map(
        on_device, mesh=mesh, in_specs=in_specs, out_specs=out_specs, check_vma=False
    )
```
